128 devices in a mesh: grp: 8 (over y, core), exp: 16 (over z, x).
Axes of the slice: x: 4, y: 4, z: 4, core: 2. Of those that a mesh axis runs over, the one named last changes fastest.
Arguments:
- tokens: bfloat16 [1536, 48, 512], P(('grp', 'exp')), parts along dimension 0, may hold values from -6 to 6
- frames: int32 [32, 4], P('grp'), parts along dimension 0, may hold values from 1 to 48, as said below
- expert_ids: int32 [73728], P(('grp', 'exp')), parts along dimension 0, may hold values from 0 to 15, as said below
- priority: int32 [73728], P(('grp', 'exp')), parts along dimension 0, may hold values from 0 to 9215, each once
- ln1_gain: float32 [512], replicated, may hold values from 0.1 to 1.9
- ln1_bias: float32 [512], replicated, may hold values from -3 to 3
- qkv_weight: bfloat16 [512, 1536], replicated
- qkv_bias: float32 [1536], replicated, may hold values from -3 to 3
- rel_bias: float32 [529, 16], replicated, may hold values from -4 to 4
- proj_weight: bfloat16 [512, 512], replicated, may hold values from -0.25 to 0.25
- proj_bias: float32 [512], replicated, may hold values from -3 to 3
- ln2_gain: float32 [512], replicated, may hold values from 0.1 to 1.9
- ln2_bias: float32 [512], replicated, may hold values from -3 to 3
- router: bfloat16 [512, 16], replicated, may hold values from -0.5 to 0.5
- fc1_weight: bfloat16 [128, 512, 2048], P(('grp', 'exp')), parts along dimension 0, may hold values from -0.25 to 0.25
- fc1_bias: float32 [128, 2048], P(('grp', 'exp')), parts along dimension 0, may hold values from -3 to 3
- fc2_weight: bfloat16 [128, 2048, 512], P(('grp', 'exp')), parts along dimension 0, may hold values from -0.125 to 0.125
- fc2_bias: float32 [128, 512], P(('grp', 'exp')), parts along dimension 0, may hold values from -3 to 3
Outputs:
- mixed: bfloat16 [1536, 48, 512], P(('grp', 'exp')), parts along dimension 0
The draws below stay inside these ranges and needn't reach their ends.
There are 8 independent parts, one for each index of `grp`. The reference program is written for one: setup_inputs(seed, part) draws one part's arguments, and reference() takes and returns one part's arrays. A program takes and returns all parts, laid end to end along the dimension named above; an argument that names none is the same for every part. Nothing has to cross between parts.
Inputs may be any that keep to these rules, and one draw needn't show every extreme that they name: `expert_ids`: among the 576 tokens of each aligned block (the rows of one device) no expert is named more than 72 times, and one expert is named exactly 72 times in every block. `priority`: each value appears once in a part. `frames`: row i: row shift and column shift of image i's windows, from 1 to 11; then its content rows, from 24 to 48; then its content columns, from 24 to 48.
All inputs are finite; a program needn't handle non-finite values.
Results may differ from the reference program's by a relative error of at most 0.0063.
Values may be sent and summed in bfloat16 or wider, within the bound.
A program may use at most 192 MiB of HBM per device.

```python
import jax
import jax.numpy as jnp
import numpy as np
from jax import lax

D = 512
HEADS = 16
HID = 2048
WIN = 12
R = 12
W = 48
H = 48
IMAGES = 4
ROWS = 192
TOK_DEV = 576
TOKENS = 9216
EXPERTS = 16
SLOTS = 72
CAP = 720
RELS = 529


def draw_frames(key, part):
    key = jax.random.fold_in(key, 5)
    key_shift, key_rows, key_cols = jax.random.split(key, 3)
    shifts = jax.random.randint(key_shift, (IMAGES, 2), 1, WIN)
    content_rows = jax.random.randint(key_rows, (IMAGES, 1), H // 2, H + 1)
    content_cols = jax.random.randint(key_cols, (IMAGES, 1), W // 2, W + 1)
    return jnp.concatenate([shifts, content_rows, content_cols], axis=1).astype(jnp.int32)


def draw_expert_ids(key, part):
    key = jax.random.fold_in(key, 11)
    key_hot, key_blocks = jax.random.split(key)
    hottest = jax.random.randint(key_hot, (), 0, EXPERTS)
    block_keys = jax.random.split(key_blocks, TOKENS // TOK_DEV)

    def one_block(block_key):
        key_order, key_warm, key_share = jax.random.split(block_key, 3)
        ranked = jax.random.permutation(key_order, TOK_DEV)
        warmer = (hottest + 1 + jax.random.randint(key_warm, (), 0, EXPERTS - 1)) % EXPERTS
        warm_count = jax.random.randint(key_share, (), SLOTS // 2, SLOTS + 1)
        lower = jnp.minimum(hottest, warmer)
        upper = jnp.maximum(hottest, warmer)
        spread = jnp.maximum(ranked - SLOTS - warm_count, 0) % (EXPERTS - 2)
        moved = spread + (spread >= lower).astype(jnp.int32)
        moved = moved + (moved >= upper).astype(jnp.int32)
        return jnp.where(ranked < SLOTS, hottest, jnp.where(ranked < SLOTS + warm_count, warmer, moved))
    return jax.vmap(one_block)(block_keys).reshape(TOKENS).astype(jnp.int32)


def draw_qkv_weight(key, part):
    key = jax.random.fold_in(key, 7)
    key_base = jax.random.fold_in(key, 0)
    full = jax.random.normal(key_base, (D, 3 * D), jnp.float32) * D ** (-0.5)
    return full.astype(jnp.bfloat16)


def steps_of(key, dims, pieces, least, top_value):
    level, own = 1.0, jax.random.fold_in(key, 6)
    for position, parts in pieces:
        heights = jnp.exp(jax.random.uniform(jax.random.fold_in(own, position), (parts,), jnp.float32, least / len(pieces), top_value / len(pieces)))
        level = level * jnp.repeat(heights, dims[position] // parts).reshape([-1 if axis == position else 1 for axis in range(len(dims))])
    return level


def scatter_about(stream_key, shape, deviation, most, cuts=(), held_as=jnp.bfloat16):
    drawn = jax.random.normal(stream_key, shape, jnp.float32) * deviation
    if len(cuts) > 0:
        drawn = steps_of(stream_key, shape, cuts, -0.22, 0.18) * drawn
    return jnp.clip(drawn, min=-most, max=most).astype(held_as)


def setup_inputs(seed: int = 0, part: int = 0) -> dict:
    seeds = jax.random.split(jax.random.key(seed), 19)
    own_keys = jax.random.split(jax.random.fold_in(seeds[18], part), 19)
    return {
        "tokens": scatter_about(own_keys[0], (ROWS, W, D), 1.0, 6.0, ((0, 16),)),
        "frames": draw_frames(jax.random.fold_in(jax.random.fold_in(seeds[18], part), 71), part),
        "expert_ids": draw_expert_ids(jax.random.fold_in(jax.random.fold_in(seeds[18], part), 71), part),
        "priority": jax.random.permutation(own_keys[3], TOKENS).astype(jnp.int32),
        "ln1_gain": jnp.clip(1.0 + 0.18 * jax.random.normal(seeds[4], (D,), jnp.float32), 0.1, 1.9),
        "ln1_bias": scatter_about(seeds[5], (D,), 0.5, 3.0, (), jnp.float32),
        "qkv_weight": draw_qkv_weight(jax.random.fold_in(seeds[18], 71), part),
        "qkv_bias": scatter_about(seeds[7], (3 * D,), 0.5, 3.0, (), jnp.float32),
        "rel_bias": scatter_about(seeds[8], (RELS, HEADS), 1.0, 4.0, (), jnp.float32),
        "proj_weight": scatter_about(seeds[9], (D, D), D ** -0.5, 0.25),
        "proj_bias": scatter_about(seeds[10], (D,), 0.5, 3.0, (), jnp.float32),
        "ln2_gain": jnp.clip(1.0 + 0.18 * jax.random.normal(seeds[11], (D,), jnp.float32), 0.1, 1.9),
        "ln2_bias": scatter_about(seeds[12], (D,), 0.5, 3.0, (), jnp.float32),
        "router": scatter_about(seeds[13], (D, EXPERTS), (D // 4) ** -0.5, 0.5),
        "fc1_weight": scatter_about(own_keys[14], (EXPERTS, D, HID), D ** -0.5, 0.25, ((0, 16),)),
        "fc1_bias": scatter_about(own_keys[15], (EXPERTS, HID), 0.5, 3.0, ((0, 16),), jnp.float32),
        "fc2_weight": scatter_about(own_keys[16], (EXPERTS, HID, D), HID ** -0.5, 0.125, ((0, 16),)),
        "fc2_bias": scatter_about(own_keys[17], (EXPERTS, D), 0.5, 3.0, ((0, 16),), jnp.float32),
    }


NEGATIVE = -1e+30

def layer_norm(values, scale_gain, shift_bias):
    widened = values.astype(jnp.float32)
    average = lax.optimization_barrier(jnp.mean(widened, axis=-1, keepdims=True))
    centred = widened - average
    variance = lax.optimization_barrier(jnp.mean(centred * centred, axis=-1, keepdims=True))
    normed = centred * lax.rsqrt(variance + 1e-05)
    return (normed * scale_gain + shift_bias).astype(jnp.bfloat16)

def relative_index():
    places = np.arange(WIN * WIN)
    across = places // WIN
    within = places % WIN
    return (across[:, None] - across[None, :] + WIN - 1) * (2 * WIN - 1) + (within[:, None] - within[None, :] + WIN - 1)

def to_windows(tensor):
    slab_rows, slab_cols = (tensor.shape[0], tensor.shape[1])
    trailing = tensor.shape[2:]
    shaped = tensor.reshape((slab_rows // WIN, WIN, slab_cols // WIN, WIN) + trailing)
    shaped = jnp.transpose(shaped, (0, 2, 1, 3) + tuple((4 + extra for extra in range(len(trailing)))))
    return shaped.reshape((slab_rows // WIN * (slab_cols // WIN), WIN * WIN) + trailing)

def from_windows(tensor, slab_rows, slab_cols):
    feature = tensor.shape[-1]
    shaped = tensor.reshape(slab_rows // WIN, slab_cols // WIN, WIN, WIN, feature)
    return jnp.transpose(shaped, (0, 2, 1, 3, 4)).reshape(slab_rows, slab_cols, feature)

def window_attend(queries, keys, values, valid_mask, region_mask, position_bias):
    slab_rows, slab_cols, model_dim = queries.shape
    head_dim = model_dim // HEADS
    query_win = to_windows(queries).reshape(-1, WIN * WIN, HEADS, head_dim).astype(jnp.float32)
    key_win = to_windows(keys).reshape(-1, WIN * WIN, HEADS, head_dim).astype(jnp.float32)
    value_win = to_windows(values).reshape(-1, WIN * WIN, HEADS, head_dim).astype(jnp.float32)
    scores = jnp.einsum('nphd,nqhd->nhpq', query_win, key_win) * head_dim ** (-0.5) + position_bias[None]
    valid_win = to_windows(valid_mask)
    region_win = to_windows(region_mask)
    allowed = valid_win[:, None, :] & (region_win[:, :, None] == region_win[:, None, :])
    scores = jnp.where(allowed[:, None], scores, NEGATIVE)
    largest = lax.optimization_barrier(jnp.max(scores, axis=-1, keepdims=True))
    expd = jnp.exp(scores - largest)
    probs = (expd / lax.optimization_barrier(jnp.sum(expd, axis=-1, keepdims=True))).astype(jnp.bfloat16)
    mixed_heads = jnp.einsum('nhpq,nqhd->nphd', probs.astype(jnp.float32), value_win).astype(jnp.bfloat16)
    return from_windows(mixed_heads.reshape(-1, WIN * WIN, model_dim), slab_rows, slab_cols)

def expert_mlp(tokens_in, first_weight, first_bias, second_weight, second_bias):
    hidden = jax.nn.gelu(jnp.dot(tokens_in, first_weight, preferred_element_type=jnp.float32) + first_bias, approximate=False).astype(jnp.bfloat16)
    return (jnp.dot(hidden, second_weight, preferred_element_type=jnp.float32) + second_bias).astype(jnp.bfloat16)

def reference(tokens, frames, expert_ids, priority, ln1_gain, ln1_bias, qkv_weight, qkv_bias, rel_bias, proj_weight, proj_bias, ln2_gain, ln2_bias, router, fc1_weight, fc1_bias, fc2_weight, fc2_bias):
    norm_one = layer_norm(tokens, ln1_gain, ln1_bias)
    image_order = jnp.roll(norm_one, 2 * R, axis=0)
    projected = jnp.dot(image_order.reshape(TOKENS, D), qkv_weight, preferred_element_type=jnp.float32) + qkv_bias
    queries = projected[:, :D].astype(jnp.bfloat16).reshape(IMAGES, H, W, D)
    keys = projected[:, D:2 * D].astype(jnp.bfloat16).reshape(IMAGES, H, W, D)
    values = projected[:, 2 * D:].astype(jnp.bfloat16).reshape(IMAGES, H, W, D)
    position_bias = jnp.transpose(rel_bias[relative_index()], (2, 0, 1))
    anchor = jnp.zeros((), jnp.int32)
    padding = ((WIN, WIN), (WIN, WIN), (0, 0))

    def one_image(packed):
        query_img, key_img, value_img, frame_row = packed
        row_shift = frame_row[0]
        col_shift = frame_row[1]
        row_pos = jnp.arange(H + 2 * WIN, dtype=jnp.int32) - WIN
        col_pos = jnp.arange(W + 2 * WIN, dtype=jnp.int32) - WIN
        valid_mask = ((row_pos >= 0) & (row_pos < H))[:, None] & ((col_pos >= 0) & (col_pos < W))[None, :]
        region_mask = (row_pos < frame_row[2])[:, None] & (col_pos < frame_row[3])[None, :]
        starts = (row_shift, col_shift, anchor)
        extent = (H + WIN, W + WIN, D)
        query_slab = lax.dynamic_slice(jnp.pad(query_img, padding), starts, extent)
        key_slab = lax.dynamic_slice(jnp.pad(key_img, padding), starts, extent)
        value_slab = lax.dynamic_slice(jnp.pad(value_img, padding), starts, extent)
        valid_slab = lax.dynamic_slice(valid_mask, (row_shift, col_shift), (H + WIN, W + WIN))
        region_slab = lax.dynamic_slice(region_mask, (row_shift, col_shift), (H + WIN, W + WIN))
        result = window_attend(query_slab, key_slab, value_slab, valid_slab, region_slab, position_bias)
        return lax.dynamic_slice(result, (WIN - row_shift, WIN - col_shift, anchor), (H, W, D))
    attended_images = lax.map(one_image, (queries, keys, values, frames))
    attended = jnp.roll(attended_images.reshape(ROWS, W, D), -2 * R, axis=0)
    flat_tokens = tokens.reshape(TOKENS, D)
    residual = (flat_tokens.astype(jnp.float32) + jnp.dot(attended.reshape(TOKENS, D), proj_weight, preferred_element_type=jnp.float32) + proj_bias).astype(jnp.bfloat16)
    norm_two = layer_norm(residual, ln2_gain, ln2_bias)
    logits = jnp.dot(norm_two, router, preferred_element_type=jnp.float32)
    gating = jax.nn.sigmoid(jnp.take_along_axis(logits, expert_ids[:, None], axis=1)[:, 0])
    expert_iota = jnp.arange(EXPERTS, dtype=jnp.int32)
    by_priority = jnp.zeros((TOKENS,), jnp.int32).at[priority].set(expert_ids)
    expert_hits = (by_priority[None, :] == expert_iota[:, None]).astype(jnp.int32)
    earlier = jnp.cumsum(expert_hits, axis=1) - expert_hits
    priority_rank = earlier[expert_ids, priority]
    keep_flag = priority_rank < CAP
    buffers = jnp.zeros((EXPERTS, CAP, D), jnp.bfloat16).at[expert_ids, priority_rank].set(norm_two, mode='drop')

    def one_expert(packed):
        return expert_mlp(packed[0], packed[1], packed[2], packed[3], packed[4])
    served = lax.map(one_expert, (buffers, fc1_weight, fc1_bias, fc2_weight, fc2_bias))
    expert_out = served[expert_ids, jnp.minimum(priority_rank, CAP - 1)]
    weight_out = jnp.where(keep_flag, gating, 0.0)
    mixed = (residual.astype(jnp.float32) + weight_out[:, None] * expert_out.astype(jnp.float32)).astype(jnp.bfloat16)
    return mixed.reshape(ROWS, W, D)
```

```python
import math
import jax
import jax.numpy as jnp
from jax import lax
from jax.experimental import pallas as pl
from jax.experimental.pallas import tpu as pltpu
from jax.sharding import PartitionSpec as P

D = 512
HEADS = 16
WIN = 12
STRIPS = 4
T = 576
SLOT = 80
CAP = 720
NEG = -1e30
ROOT = math.sqrt(32.0)
EXPC = math.log2(math.e) / ROOT
F32, BF16, I32 = jnp.float32, jnp.bfloat16, jnp.int32


def iota(shape, dim):
    return lax.broadcasted_iota(I32, shape, dim)


def dot(a, b, dims=((1,), (0,))):
    return lax.dot_general(a, b, (dims, ((), ())), preferred_element_type=F32)


def norm(x, gain, bias):
    mean = jnp.mean(x, axis=-1, keepdims=True)
    c = x - mean
    var = jnp.mean(c * c, axis=-1, keepdims=True)
    return (c * lax.rsqrt(var + 1e-5) * gain + bias).astype(BF16)


def column(row):
    return jnp.transpose(jnp.broadcast_to(row, (128, row.shape[1])))[:, :1]


def build_perm(perm, sr, sc):
    p = iota((T, 1), 0)
    j = p // 144
    w = p - j * 144
    rt = w // 12
    ct = w - rt * 12
    m = rt + sr
    m = jnp.where(m >= 12, m - 12, m)
    c = 12 * j + ct + sc
    c = jnp.where(c >= 48, c - 48, c)
    t = m * 48 + c
    perm[...] = jnp.where(iota((T, T), 1) == t, 1.0, 0.0).astype(BF16)


def build_bias(rel, shifted, spread, table):
    r16 = rel[...]
    for r in range(24):
        half, cu = divmod(r, 12)
        s = (-(11 - cu - 23 * half)) % 640
        x = pltpu.roll(r16, s, 1) if s else r16
        hi = x.astype(BF16)
        lo = (x - hi.astype(F32)).astype(BF16)
        shifted[16 * r : 16 * r + 16, :] = hi
        shifted[384 + 16 * r : 384 + 16 * r + 16, :] = lo
    lane = iota((1, 384), 1)
    dr = lane // 12
    want = jnp.where(lane < 276, dr * 23 + lane - dr * 12, -1)
    sel = jnp.where(iota((640, 384), 0) == want, 1.0, 0.0).astype(BF16)
    full = dot(shifted[...], sel)
    full = full[:384] + full[384:]
    for i in range(3):
        spread[i] = full[:, 128 * i : 128 * i + 128]
    for h in range(HEADS):
        g, hh = divmod(h, 4)
        rows = jnp.concatenate([spread[i, pl.ds(h, 24, stride=16), :] for i in range(3)], axis=1)
        for i in range(6):
            start = (11 - 2 * i) * 12
            table[g, 24 * i : 24 * i + 24, 128 * hh : 128 * hh + 128] = rows[:, start : start + 128]
            table[g, 24 * i : 24 * i + 24, 512 + 16 * hh : 528 + 16 * hh] = rows[:, start + 128 : start + 144]


def project_own(xop, wqkv, qkvb, sr, qbd, ko, vo):
    k = dot(xop, wqkv[:, D : 2 * D]) + qkvb[:, D : 2 * D]
    ko[...] = k.astype(BF16)
    bq = column(qkvb[:, :D])
    bv = column(qkvb[:, 2 * D :])
    lane_rt = iota((1, 144), 1) // 12
    in_a = lane_rt >= 12 - sr
    qbd[...] = jnp.zeros_like(qbd)
    for j in range(4):
        xj = xop[144 * j : 144 * j + 144, :]
        qt = dot(wqkv[:, :D], xj, ((0,), (1,))) + bq
        qa = jnp.where(in_a, qt, 0.0).astype(BF16)
        qb = jnp.where(in_a, 0.0, qt).astype(BF16)
        for h in range(HEADS):
            g, hh = divmod(h, 4)
            f = slice(32 * h, 32 * h + 32)
            for off, q in ((0, qa), (128, qb)):
                r = slice(off + 32 * hh, off + 32 * hh + 32)
                qbd[4 * j + g, r, 128 * hh : 128 * hh + 128] = q[f, :128]
                qbd[4 * j + g, r, 512 + 16 * hh : 528 + 16 * hh] = q[f, 128:]
        vo[j] = (dot(wqkv[:, 2 * D :], xj, ((0,), (1,))) + bv).astype(BF16)


def project_halo(xhp, wqkv, qkvb, sr, ko, vo, kab, vab):
    bv = column(qkvb[:, 2 * D :])
    p = iota((T, 1), 0)
    w = p - (p // 144) * 144
    row_a = w // 12 >= 12 - sr
    kh = (dot(xhp, wqkv[:, D : 2 * D]) + qkvb[:, D : 2 * D]).astype(BF16).astype(F32)
    kof = ko[...].astype(F32)
    ka = jnp.where(row_a, kof, kh).astype(BF16)
    kb = jnp.where(row_a, kh, kof).astype(BF16)
    for g in range(4):
        kab[:, 256 * g : 256 * g + 128] = ka[:, 128 * g : 128 * g + 128]
        kab[:, 256 * g + 128 : 256 * g + 256] = kb[:, 128 * g : 128 * g + 128]
    in_a = iota((1, 144), 1) // 12 >= 12 - sr
    for j in range(4):
        xj = xhp[144 * j : 144 * j + 144, :]
        vh = (dot(wqkv[:, 2 * D :], xj, ((0,), (1,))) + bv).astype(BF16).astype(F32)
        vof = vo[j].astype(F32)
        va = jnp.where(in_a, vof, vh).astype(BF16)
        vb = jnp.where(in_a, vh, vof).astype(BF16)
        for h in range(HEADS):
            vab[j, 64 * h : 64 * h + 32, :] = va[32 * h : 32 * h + 32, :]
            vab[j, 64 * h + 32 : 64 * h + 64, :] = vb[32 * h : 32 * h + 32, :]


def attend(j, strip, sr, sc, rows_in, cols_in, qbd, kab, vab, table, att):
    base = strip * 12 + sr

    def cols_of(w):
        ct = w - (w // 12) * 12
        c = 12 * j + ct + sc
        wrapped = c >= 48
        return jnp.where(wrapped, c - 48, c), wrapped

    kpos = iota((144, 1), 0)
    kr = kpos // 12
    kc, kwrap = cols_of(kpos)

    def gid(row, col, wrap):
        region = jnp.where(row < rows_in, jnp.where(col < cols_in, 1, 0), 0)
        return region + jnp.where(wrap, 2, 0)

    row_ka = base - 12 + kr
    row_kb = base + kr
    gid_ka = jnp.where(row_ka < 0, -1, gid(row_ka, kc, kwrap))
    gid_kb = jnp.where(row_kb >= 48, -1, gid(row_kb, kc, kwrap))

    def masks(qpos):
        qr = qpos // 12
        qa = qr >= 12 - sr
        qc, qwrap = cols_of(qpos)
        row_q = jnp.where(qa, base - 12 + qr, base + qr)
        gq = gid(row_q, qc, qwrap)
        want = jnp.where(qa, gid_ka, gid_kb)
        return qa, jnp.where(want == gq, 0.0, NEG)

    lane = iota((1, 128), 1)
    qa_main, m_main = masks(lane)
    lane64 = iota((1, 64), 1)
    qa_rem, m_rem = masks(128 + lane64 - (lane64 // 16) * 16)

    def softmax(s):
        e = jnp.exp2((s - jnp.max(s, axis=0, keepdims=True)) * EXPC)
        return e.astype(BF16), 1.0 / jnp.sum(e, axis=0, keepdims=True)

    for g in range(4):
        s = dot(kab[pl.ds(144 * j, 144), 256 * g : 256 * g + 256], qbd[4 * j + g])
        for hh in range(4):
            h = 4 * g + hh
            sl = slice(128 * hh, 128 * hh + 128)
            e, inv = softmax(s[:, sl] + table[g, :, sl] + m_main)
            o = dot(vab[j, 64 * h : 64 * h + 64, :], e)
            o = jnp.where(qa_main, o[:32], o[32:]) * inv
            att[j, 32 * h : 32 * h + 32, :128] = o.astype(BF16)
        e, inv = softmax(s[:, 512:576] + table[g, :, 512:576] + m_rem)
        o = dot(vab[j, 256 * g : 256 * g + 256, :], e)
        for hh in range(4):
            h = 4 * g + hh
            part = jnp.where(qa_rem, o[64 * hh : 64 * hh + 32], o[64 * hh + 32 : 64 * hh + 64]) * inv
            att[j, 32 * h : 32 * h + 32, 128:144] = part[:, 16 * hh : 16 * hh + 16].astype(BF16)


def after_attention(att, perm, tokens, wp, bp, g2, b2):
    acc = dot(att[0], perm[0:144, :])
    for j in range(1, 4):
        acc += dot(att[j], perm[144 * j : 144 * j + 144, :])
    projected = dot(acc.astype(BF16), wp, ((0,), (0,))) + bp
    residual = (tokens.astype(F32) + projected).astype(BF16)
    return residual, norm(residual.astype(F32), g2, b2)


def slot_row(ids_row):
    hits = jnp.where(ids_row == iota((16, T), 0), 1.0, 0.0)
    upper = jnp.where(iota((T, T), 0) < iota((T, T), 1), 1.0, 0.0).astype(BF16)
    before = dot(hits.astype(BF16), upper)
    slot = jnp.sum(before * hits, axis=0, keepdims=True)
    return ids_row * SLOT + slot.astype(I32)


def slot_col(ids_col):
    hits = jnp.where(ids_col == iota((T, 16), 1), 1.0, 0.0)
    lower = jnp.where(iota((T, T), 1) < iota((T, T), 0), 1.0, 0.0).astype(BF16)
    before = dot(lower, hits.astype(BF16))
    slot = jnp.sum(before * hits, axis=1, keepdims=True)
    return ids_col * SLOT + slot.astype(I32)


def thresholds(all_ids, all_pri, masked):
    for s in range(16):
        masked[s] = jnp.where(all_ids[s : s + 1, :] == iota((16, T), 0), all_pri[s : s + 1, :], 1 << 20)

    def step(i, x):
        cand = x + lax.shift_left(jnp.int32(1), 13 - i)
        count = jnp.zeros((16, T), I32)
        for s in range(16):
            count += jnp.where(masked[s] < cand, 1, 0)
        total = jnp.sum(count.astype(F32), axis=1, keepdims=True)
        return jnp.where(total <= CAP - 1.0, cand, x)

    return lax.fori_loop(0, 14, step, jnp.zeros((16, 1), I32))


def weight_col(norm2, router, ids_col, pri_col, limit):
    logits = dot(norm2, router)
    hits = ids_col == iota((T, 16), 1)
    gate = 1.0 / (1.0 + jnp.exp(-jnp.sum(jnp.where(hits, logits, 0.0), axis=1, keepdims=True)))
    limit_row = jnp.sum(jnp.where(iota((16, 16), 0) == iota((16, 16), 1), limit.astype(F32), 0.0), axis=0, keepdims=True)
    own_limit = jnp.sum(jnp.where(hits, limit_row, 0.0), axis=1, keepdims=True)
    return jnp.where(pri_col.astype(F32) <= own_limit, gate, 0.0)


def gelu(x):
    z = jnp.abs(x)
    t = 1.0 / (1.0 + (0.3275911 / math.sqrt(2.0)) * z)
    poly = 0.5 * 1.061405429
    for a in (-1.453152027, 1.421413741, -0.284496736, 0.254829592):
        poly = poly * t + 0.5 * a
    tail = poly * t * jnp.exp2((-0.5 * math.log2(math.e)) * (x * x))
    return jnp.maximum(x, 0.0) - z * tail


def mlp(x, w1, b1, w2, b2, step=512):
    acc = None
    for c in range(0, 2048, step):
        h = gelu(dot(x, w1[:, c : c + step]) + b1[:, c : c + step]).astype(BF16)
        y = dot(h, w2[c : c + step, :])
        acc = y if acc is None else acc + y
    return (acc + b2).astype(BF16)


def front_kernel(
    frames, tokens, prev, following, ids_row, ids_col, pri_col, all_ids, all_pri, g1, b1, wqkv, qkvb, rel, wp, bp, g2, b2, router,
    outgoing, residual_ref, weight_ref,
    perm, shifted, spread, table, qbd, ko, vo, kab, vab, att, masked,
):
    device = lax.axis_index("exp")
    strip_all = lax.rem(device + 2, 16)
    image = strip_all // STRIPS
    strip = lax.rem(strip_all, STRIPS)
    sr, sc, rows_in, cols_in = (frames[image, i] for i in range(4))
    build_perm(perm, sr, sc)
    build_bias(rel, shifted, spread, table)
    own = norm(tokens[...].astype(F32), g1[...], b1[...])
    xop = dot(perm[...], own).astype(BF16)
    project_own(xop, wqkv, qkvb, sr, qbd, ko, vo)
    limit = thresholds(all_ids, all_pri, masked)
    low = iota((T, 1), 0) // 48 < sr
    halo = jnp.where(low, following[...].astype(F32), prev[...].astype(F32))
    have = jnp.where(low, jnp.where(strip < 3, 1, 0), jnp.where(strip > 0, 1, 0)) > 0
    halo = norm(jnp.where(have, halo, 0.0), g1[...], b1[...])
    xhp = dot(perm[...], halo).astype(BF16)
    project_halo(xhp, wqkv, qkvb, sr, ko, vo, kab, vab)

    def window(j, carry):
        attend(j, strip, sr, sc, rows_in, cols_in, qbd, kab, vab, table, att)
        return carry

    lax.fori_loop(0, 4, window, 0)
    residual, norm2 = after_attention(att, perm, tokens[...], wp[...], bp[...], g2[...], b2[...])
    residual_ref[...] = residual
    weight_ref[...] = weight_col(norm2, router[...], ids_col[...], pri_col[...], limit)
    dest = slot_row(ids_row[...])
    for e in range(16):
        pick = jnp.where(iota((SLOT, T), 0) + SLOT * e == dest, 1.0, 0.0).astype(BF16)
        outgoing[e] = dot(pick, norm2).astype(BF16)


def mlp_kernel(x, w1, b1, w2, b2, y):
    for c in range(4):
        xin = x[4 * c : 4 * c + 4].reshape(4 * SLOT, D)
        y[4 * c : 4 * c + 4] = mlp(xin, w1, b1, w2, b2[...]).reshape(4, SLOT, D)


def combine_kernel(returned, ids_col, residual, weight, out):
    dest = slot_col(ids_col[...])
    pick = jnp.where(iota((T, 16 * SLOT), 1) == dest, 1.0, 0.0).astype(BF16)
    e = dot(pick, returned[...])
    out[...] = (residual[...].astype(F32) + weight[...] * e).astype(BF16)


def shards(tokens, frames, ids, pri, g1, b1, wqkv, qkvb, rel_bias, wp, bp, g2, b2, router, f1, f1b, f2, f2b):
    params = pltpu.CompilerParams(vmem_limit_bytes=60 * 1024 * 1024)
    flat = tokens.reshape(T, D)
    n = lax.axis_size("exp")
    up = [(i, (i + 1) % n) for i in range(n)]
    down = [(j, i) for i, j in up]
    prev = lax.ppermute(flat, "exp", up)
    following = lax.ppermute(flat, "exp", down)
    both = lax.all_gather(jnp.stack([ids, pri]), "exp", axis=0)
    all_ids, all_pri = both[:, 0], both[:, 1]
    row = lambda v: v.reshape(1, -1)
    rel = jnp.pad(rel_bias.T * ROOT, ((0, 0), (0, 640 - 529)))
    ids_col = ids.reshape(T, 1)
    vm = pl.BlockSpec(memory_space=pltpu.VMEM)
    outgoing, residual, weight = pl.pallas_call(
        front_kernel,
        out_shape=(
            jax.ShapeDtypeStruct((16, SLOT, D), BF16),
            jax.ShapeDtypeStruct((T, D), BF16),
            jax.ShapeDtypeStruct((T, 1), F32),
        ),
        in_specs=[pl.BlockSpec(memory_space=pltpu.SMEM)] + [vm] * 18,
        out_specs=(vm, vm, vm),
        scratch_shapes=[
            pltpu.VMEM((T, T), BF16),
            pltpu.VMEM((768, 640), BF16),
            pltpu.VMEM((3, 384, 128), F32),
            pltpu.VMEM((4, 144, T), F32),
            pltpu.VMEM((16, 256, T), BF16),
            pltpu.VMEM((T, D), BF16),
            pltpu.VMEM((4, D, 144), BF16),
            pltpu.VMEM((T, 2 * D), BF16),
            pltpu.VMEM((4, 2 * D, 144), BF16),
            pltpu.VMEM((4, D, 144), BF16),
            pltpu.VMEM((16, 16, T), I32),
        ],
        compiler_params=params,
    )(frames, flat, prev, following, row(ids), ids_col, pri.reshape(T, 1), all_ids, all_pri, row(g1), row(b1), wqkv, row(qkvb), rel, wp, row(bp), row(g2), row(b2), router)
    incoming = lax.all_to_all(outgoing, "exp", split_axis=0, concat_axis=0, tiled=True)
    served = pl.pallas_call(
        mlp_kernel,
        out_shape=jax.ShapeDtypeStruct((16, SLOT, D), BF16),
        in_specs=[vm] * 5,
        out_specs=vm,
        compiler_params=params,
    )(incoming, f1[0], row(f1b[0]), f2[0], row(f2b[0]))
    returned = lax.all_to_all(served, "exp", split_axis=0, concat_axis=0, tiled=True)
    out = pl.pallas_call(
        combine_kernel,
        out_shape=jax.ShapeDtypeStruct((T, D), BF16),
        in_specs=[vm] * 4,
        out_specs=vm,
        compiler_params=params,
    )(returned.reshape(16 * SLOT, D), ids_col, residual, weight)
    return out.reshape(tokens.shape)


def solution(mesh):
    both = ("grp", "exp")
    one = P(both)
    rep = P()
    in_specs = (P(both, None, None), P("grp", None), one, one) + (rep,) * 10 + (
        P(both, None, None), P(both, None), P(both, None, None), P(both, None))
    return jax.shard_map(shards, mesh=mesh, in_specs=in_specs, out_specs=P(both, None, None), check_vma=False)
```

```python
import math
import jax
import jax.numpy as jnp
from jax import lax
from jax.experimental import pallas as pl
from jax.experimental.pallas import tpu as pltpu
from jax.sharding import PartitionSpec as P

D = 512
HEADS = 16
WIN = 12
STRIPS = 4
T = 576
SLOT = 80
CAP = 720
NEG = -1e30
ROOT = math.sqrt(32.0)
EXPC = math.log2(math.e) / ROOT
F32, BF16, I32 = jnp.float32, jnp.bfloat16, jnp.int32


def iota(shape, dim):
    return lax.broadcasted_iota(I32, shape, dim)


def dot(a, b, dims=((1,), (0,))):
    return lax.dot_general(a, b, (dims, ((), ())), preferred_element_type=F32)


def norm(x, gain, bias):
    mean = jnp.mean(x, axis=-1, keepdims=True)
    c = x - mean
    var = jnp.mean(c * c, axis=-1, keepdims=True)
    return (c * lax.rsqrt(var + 1e-5) * gain + bias).astype(BF16)


def column(row):
    n = row.shape[1]
    if n % 128:
        row = jnp.concatenate([row, jnp.zeros((1, -n % 128), row.dtype)], axis=1)
    return jnp.transpose(jnp.broadcast_to(row, (128, row.shape[1])))[:n, :1]


def build_perm(perm, sr, sc):
    p = iota((T, 1), 0)
    j = p // 144
    w = p - j * 144
    rt = w // 12
    ct = w - rt * 12
    m = rt + sr
    m = jnp.where(m >= 12, m - 12, m)
    c = 12 * j + ct + sc
    c = jnp.where(c >= 48, c - 48, c)
    t = m * 48 + c
    perm[...] = jnp.where(iota((T, T), 1) == t, 1.0, 0.0).astype(BF16)


def build_bias(rel, shifted, spread, table):
    r16 = jnp.concatenate([rel[...] * ROOT, jnp.zeros((16, 640 - 529), F32)], axis=1)
    for r in range(24):
        half, cu = divmod(r, 12)
        s = (-(11 - cu - 23 * half)) % 640
        x = pltpu.roll(r16, s, 1) if s else r16
        hi = x.astype(BF16)
        lo = (x - hi.astype(F32)).astype(BF16)
        shifted[16 * r : 16 * r + 16, :] = hi
        shifted[384 + 16 * r : 384 + 16 * r + 16, :] = lo
    lane = iota((1, 384), 1)
    dr = lane // 12
    want = jnp.where(lane < 276, dr * 23 + lane - dr * 12, -1)
    sel = jnp.where(iota((640, 384), 0) == want, 1.0, 0.0).astype(BF16)
    full = dot(shifted[...], sel)
    full = full[:384] + full[384:]
    for i in range(3):
        spread[i] = full[:, 128 * i : 128 * i + 128]
    for h in range(HEADS):
        g, hh = divmod(h, 4)
        rows = jnp.concatenate([spread[i, pl.ds(h, 24, stride=16), :] for i in range(3)], axis=1)
        for i in range(6):
            start = (11 - 2 * i) * 12
            table[g, 24 * i : 24 * i + 24, 128 * hh : 128 * hh + 128] = rows[:, start : start + 128]
            table[g, 24 * i : 24 * i + 24, 512 + 16 * hh : 528 + 16 * hh] = rows[:, start + 128 : start + 144]


def project_own(xop, wqkv, qkvb, sr, qbd, ko, vo):
    k = dot(xop, wqkv[:, D : 2 * D]) + qkvb[:, D : 2 * D]
    ko[...] = k.astype(BF16)
    bq = column(qkvb[:, :D])
    bv = column(qkvb[:, 2 * D :])
    lane_rt = iota((1, 144), 1) // 12
    in_a = lane_rt >= 12 - sr
    qbd[...] = jnp.zeros_like(qbd)
    for j in range(4):
        xj = xop[144 * j : 144 * j + 144, :]
        qt = dot(wqkv[:, :D], xj, ((0,), (1,))) + bq
        qa = jnp.where(in_a, qt, 0.0).astype(BF16)
        qb = jnp.where(in_a, 0.0, qt).astype(BF16)
        for h in range(HEADS):
            g, hh = divmod(h, 4)
            f = slice(32 * h, 32 * h + 32)
            for off, q in ((0, qa), (128, qb)):
                r = slice(off + 32 * hh, off + 32 * hh + 32)
                qbd[4 * j + g, r, 128 * hh : 128 * hh + 128] = q[f, :128]
                qbd[4 * j + g, r, 512 + 16 * hh : 528 + 16 * hh] = q[f, 128:]
        vo[j] = (dot(wqkv[:, 2 * D :], xj, ((0,), (1,))) + bv).astype(BF16)


def project_halo(xhp, wqkv, qkvb, sr, ko, vo, kab, vab):
    bv = column(qkvb[:, 2 * D :])
    p = iota((T, 1), 0)
    w = p - (p // 144) * 144
    row_a = w // 12 >= 12 - sr
    kh = (dot(xhp, wqkv[:, D : 2 * D]) + qkvb[:, D : 2 * D]).astype(BF16).astype(F32)
    kof = ko[...].astype(F32)
    ka = jnp.where(row_a, kof, kh).astype(BF16)
    kb = jnp.where(row_a, kh, kof).astype(BF16)
    for g in range(4):
        kab[:, 256 * g : 256 * g + 128] = ka[:, 128 * g : 128 * g + 128]
        kab[:, 256 * g + 128 : 256 * g + 256] = kb[:, 128 * g : 128 * g + 128]
    in_a = iota((1, 144), 1) // 12 >= 12 - sr
    for j in range(4):
        xj = xhp[144 * j : 144 * j + 144, :]
        vh = (dot(wqkv[:, 2 * D :], xj, ((0,), (1,))) + bv).astype(BF16).astype(F32)
        vof = vo[j].astype(F32)
        va = jnp.where(in_a, vof, vh).astype(BF16)
        vb = jnp.where(in_a, vh, vof).astype(BF16)
        for h in range(HEADS):
            vab[j, 64 * h : 64 * h + 32, :] = va[32 * h : 32 * h + 32, :]
            vab[j, 64 * h + 32 : 64 * h + 64, :] = vb[32 * h : 32 * h + 32, :]


def attend(j, strip, sr, sc, rows_in, cols_in, qbd, kab, vab, table, att):
    base = strip * 12 + sr

    def cols_of(w):
        ct = w - (w // 12) * 12
        c = 12 * j + ct + sc
        wrapped = c >= 48
        return jnp.where(wrapped, c - 48, c), wrapped

    kpos = iota((144, 1), 0)
    kr = kpos // 12
    kc, kwrap = cols_of(kpos)

    def gid(row, col, wrap):
        region = jnp.where(row < rows_in, jnp.where(col < cols_in, 1, 0), 0)
        return region + jnp.where(wrap, 2, 0)

    row_ka = base - 12 + kr
    row_kb = base + kr
    gid_ka = jnp.where(row_ka < 0, -1, gid(row_ka, kc, kwrap))
    gid_kb = jnp.where(row_kb >= 48, -1, gid(row_kb, kc, kwrap))

    def masks(qpos):
        qr = qpos // 12
        qa = qr >= 12 - sr
        qc, qwrap = cols_of(qpos)
        row_q = jnp.where(qa, base - 12 + qr, base + qr)
        gq = gid(row_q, qc, qwrap)
        want = jnp.where(qa, gid_ka, gid_kb)
        return qa, jnp.where(want == gq, 0.0, NEG)

    lane = iota((1, 128), 1)
    qa_main, m_main = masks(lane)
    lane64 = iota((1, 64), 1)
    qa_rem, m_rem = masks(128 + lane64 - (lane64 // 16) * 16)

    def softmax(s):
        e = jnp.exp2((s - jnp.max(s, axis=0, keepdims=True)) * EXPC)
        return e.astype(BF16), 1.0 / jnp.sum(e, axis=0, keepdims=True)

    for g in range(4):
        s = dot(kab[pl.ds(144 * j, 144), 256 * g : 256 * g + 256], qbd[4 * j + g])
        for hh in range(4):
            h = 4 * g + hh
            sl = slice(128 * hh, 128 * hh + 128)
            e, inv = softmax(s[:, sl] + table[g, :, sl] + m_main)
            o = dot(vab[j, 64 * h : 64 * h + 64, :], e)
            o = jnp.where(qa_main, o[:32], o[32:]) * inv
            att[j, 32 * h : 32 * h + 32, :128] = o.astype(BF16)
        e, inv = softmax(s[:, 512:576] + table[g, :, 512:576] + m_rem)
        o = dot(vab[j, 256 * g : 256 * g + 256, :], e)
        for hh in range(4):
            h = 4 * g + hh
            part = jnp.where(qa_rem, o[64 * hh : 64 * hh + 32], o[64 * hh + 32 : 64 * hh + 64]) * inv
            att[j, 32 * h : 32 * h + 32, 128:144] = part[:, 16 * hh : 16 * hh + 16].astype(BF16)


def after_attention(att, perm, tokens, wp, bp, g2, b2):
    acc = dot(att[0], perm[0:144, :])
    for j in range(1, 4):
        acc += dot(att[j], perm[144 * j : 144 * j + 144, :])
    projected = dot(acc.astype(BF16), wp, ((0,), (0,))) + bp
    residual = (tokens.astype(F32) + projected).astype(BF16)
    return residual, norm(residual.astype(F32), g2, b2)


def slot_row(ids_row):
    hits = jnp.where(ids_row == iota((16, T), 0), 1.0, 0.0)
    upper = jnp.where(iota((T, T), 0) < iota((T, T), 1), 1.0, 0.0).astype(BF16)
    before = dot(hits.astype(BF16), upper)
    slot = jnp.sum(before * hits, axis=0, keepdims=True)
    return ids_row * SLOT + slot.astype(I32)


def slot_col(ids_col):
    hits = jnp.where(ids_col == iota((T, 16), 1), 1.0, 0.0)
    lower = jnp.where(iota((T, T), 1) < iota((T, T), 0), 1.0, 0.0).astype(BF16)
    before = dot(lower, hits.astype(BF16))
    slot = jnp.sum(before * hits, axis=1, keepdims=True)
    return ids_col * SLOT + slot.astype(I32)


def thresholds(gathered, masked):
    for s in range(16):
        masked[s] = jnp.where(gathered[s, 0:1, :] == iota((16, T), 0), gathered[s, 1:2, :], 1 << 20)

    def step(i, x):
        cand = x + lax.shift_left(jnp.int32(1), 13 - i)
        count = jnp.zeros((16, T), I32)
        for s in range(16):
            count += jnp.where(masked[s] < cand, 1, 0)
        total = jnp.sum(count.astype(F32), axis=1, keepdims=True)
        return jnp.where(total <= CAP - 1.0, cand, x)

    return lax.fori_loop(0, 14, step, jnp.zeros((16, 1), I32))


def weight_col(norm2, router, ids_col, pri_col, limit):
    logits = dot(norm2, router, ((1,), (1,)))
    hits = ids_col == iota((T, 16), 1)
    gate = 1.0 / (1.0 + jnp.exp(-jnp.sum(jnp.where(hits, logits, 0.0), axis=1, keepdims=True)))
    limit_row = jnp.sum(jnp.where(iota((16, 16), 0) == iota((16, 16), 1), limit.astype(F32), 0.0), axis=0, keepdims=True)
    own_limit = jnp.sum(jnp.where(hits, limit_row, 0.0), axis=1, keepdims=True)
    return jnp.where(pri_col.astype(F32) <= own_limit, gate, 0.0)


def gelu(x):
    z = jnp.abs(x)
    t = 1.0 / (1.0 + (0.3275911 / math.sqrt(2.0)) * z)
    poly = 0.5 * 1.061405429
    for a in (-1.453152027, 1.421413741, -0.284496736, 0.254829592):
        poly = poly * t + 0.5 * a
    tail = poly * t * jnp.exp2((-0.5 * math.log2(math.e)) * (x * x))
    return jnp.maximum(x, 0.0) - z * tail


def mlp(x, w1, b1, w2, b2, step=512):
    acc = None
    for c in range(0, 2048, step):
        h = gelu(dot(x, w1[:, c : c + step]) + b1[:, c : c + step]).astype(BF16)
        y = dot(h, w2[c : c + step, :])
        acc = y if acc is None else acc + y
    return (acc + b2).astype(BF16)


def remote(src, dst, send, recv, target):
    return pltpu.make_async_remote_copy(
        src_ref=src, dst_ref=dst, send_sem=send, recv_sem=recv,
        device_id={"exp": target}, device_id_type=pl.DeviceIdType.MESH)


def block_kernel(
    frames, tokens_any, ids1, pri1, g1, b1, wqkv_any, qkvb, rel, wp_any, bp, g2, b2, router, f1_any, f1b, f2_any, f2b,
    out,
    tokens, prev, following, gathered, wqkv, wp, w1, w2,
    perm, shifted, spread, table, qbd, ko, vo, kab, vab, att, masked, residual, outgoing, incoming, served, returned,
    local, halo_send, halo_recv, ids_send, ids_recv, go_send, go_recv, back_send, back_recv,
):
    me = lax.axis_index("exp")
    strip_all = lax.rem(me + 2, 16)
    image = strip_all // STRIPS
    strip = lax.rem(strip_all, STRIPS)
    right, left = lax.rem(me + 1, 16), lax.rem(me + 15, 16)
    barrier = pltpu.get_barrier_semaphore()
    for d in range(1, 16):
        pl.semaphore_signal(barrier, inc=1, device_id={"exp": lax.rem(me + d, 16)}, device_id_type=pl.DeviceIdType.MESH)
    loads = [
        pltpu.make_async_copy(src, dst, local.at[i])
        for i, (src, dst) in enumerate(((tokens_any, tokens), (wqkv_any, wqkv), (wp_any, wp), (f1_any, w1), (f2_any, w2)))
    ]
    for load in loads:
        load.start()
    row = lambda ref: ref[...].reshape(1, ref.shape[0])
    ids_row, pri_row = row(ids1), row(pri1)
    gathered[0, 0:1, :] = ids_row
    gathered[0, 1:2, :] = pri_row
    pl.semaphore_wait(barrier, 15)

    n = 11 * 48
    to_left = remote(tokens_any.at[pl.ds(0, n)], following.at[pl.ds(0, n)], halo_send.at[0], halo_recv.at[0], left)
    to_right = remote(tokens_any.at[pl.ds(48, n)], prev.at[pl.ds(48, n)], halo_send.at[1], halo_recv.at[1], right)

    @pl.when(strip > 0)
    def _():
        to_left.start()

    @pl.when(strip < 3)
    def _():
        to_right.start()

    ids_copies = [
        remote(gathered.at[0], gathered.at[d], ids_send.at[d - 1], ids_recv.at[d - 1], lax.rem(me + d, 16))
        for d in range(1, 16)
    ]
    for copy in ids_copies:
        copy.start()

    sr, sc, rows_in, cols_in = (frames[image, i] for i in range(4))
    gain1, bias1 = row(g1), row(b1)
    qkv_row = row(qkvb)
    build_perm(perm, sr, sc)
    loads[0].wait()
    own = norm(tokens[...].astype(F32), gain1, bias1)
    xop = dot(perm[...], own).astype(BF16)
    loads[1].wait()
    project_own(xop, wqkv, qkv_row, sr, qbd, ko, vo)
    build_bias(rel, shifted, spread, table)
    for copy in ids_copies:
        copy.wait_recv()
    limit = thresholds(gathered, masked)

    @pl.when(strip < 3)
    def _():
        to_left.wait_recv()

    @pl.when(strip > 0)
    def _():
        to_right.wait_recv()

    low = iota((T, 1), 0) // 48 < sr
    middle = jnp.where(low[48:n], following[48:n, :].astype(F32), prev[48:n, :].astype(F32))
    halo = jnp.concatenate([following[:48, :].astype(F32), middle, prev[n:, :].astype(F32)], axis=0)
    have = jnp.where(low, jnp.where(strip < 3, 1, 0), jnp.where(strip > 0, 1, 0)) > 0
    halo = norm(jnp.where(have, halo, 0.0), gain1, bias1)
    xhp = dot(perm[...], halo).astype(BF16)
    project_halo(xhp, wqkv, qkv_row, sr, ko, vo, kab, vab)

    def window(j, carry):
        attend(j, strip, sr, sc, rows_in, cols_in, qbd, kab, vab, table, att)
        return carry

    lax.fori_loop(0, 4, window, 0)
    loads[2].wait()
    res, norm2 = after_attention(att, perm, tokens[...], wp[...], row(bp), row(g2), row(b2))
    residual[...] = res

    relative = lax.rem(ids_row - me + 16, 16)
    dest = slot_row(relative)
    go = [None] + [
        remote(outgoing.at[d], incoming.at[d], go_send.at[d - 1], go_recv.at[d - 1], lax.rem(me + d, 16))
        for d in range(1, 16)
    ]
    back = [None] + [
        remote(served.at[d], returned.at[d], back_send.at[d - 1], back_recv.at[d - 1], lax.rem(me - d + 16, 16))
        for d in range(1, 16)
    ]
    for c in range(4):
        pick = jnp.where(iota((4 * SLOT, T), 0) + 4 * SLOT * c == dest, 1.0, 0.0).astype(BF16)
        outgoing[4 * c : 4 * c + 4] = dot(pick, norm2).astype(BF16).reshape(4, SLOT, D)
        for d in range(4 * c, 4 * c + 4):
            if d:
                go[d].start()
    ids_col, pri_col = column(ids_row.astype(F32)).astype(I32), column(pri_row.astype(F32))
    weight = weight_col(norm2, router[...], ids_col, pri_col, limit)
    dest_col = slot_col(lax.rem(ids_col - me + 16, 16))
    loads[3].wait()
    loads[4].wait()
    for c in range(4):
        for d in range(4 * c, 4 * c + 4):
            if d:
                go[d].wait_recv()
        if c:
            x = incoming[4 * c : 4 * c + 4]
        else:
            x = jnp.concatenate([outgoing[0:1], incoming[1:4]], axis=0)
        y = mlp(x.reshape(4 * SLOT, D), w1, f1b, w2, f2b[...]).reshape(4, SLOT, D)
        if c:
            served[4 * c : 4 * c + 4] = y
        else:
            returned[0] = y[0]
            served[1:4] = y[1:4]
        for d in range(4 * c, 4 * c + 4):
            if d:
                back[d].start()
    pick = jnp.where(iota((T, 16 * SLOT), 1) == dest_col, 1.0, 0.0).astype(BF16)
    for d in range(1, 16):
        back[d].wait_recv()
    e = dot(pick, returned[...].reshape(16 * SLOT, D))
    out[...] = (residual[...].astype(F32) + weight * e).astype(BF16)

    @pl.when(strip > 0)
    def _():
        to_left.wait_send()

    @pl.when(strip < 3)
    def _():
        to_right.wait_send()

    for copy in ids_copies + go[1:] + back[1:]:
        copy.wait_send()


def shards(tokens, frames, ids, pri, g1, b1, wqkv, qkvb, rel_bias, wp, bp, g2, b2, router, f1, f1b, f2, f2b):
    vm = pl.BlockSpec(memory_space=pltpu.VMEM)
    hbm = pl.BlockSpec(memory_space=pl.ANY)
    specs = [pl.BlockSpec(memory_space=pltpu.SMEM), hbm, vm, vm, vm, vm, hbm, vm, vm, hbm, vm, vm, vm, vm, hbm, vm, hbm, vm]
    dma = pltpu.SemaphoreType.DMA
    out = pl.pallas_call(
        block_kernel,
        out_shape=jax.ShapeDtypeStruct((T, D), BF16),
        in_specs=specs,
        out_specs=vm,
        scratch_shapes=[
            pltpu.VMEM((T, D), BF16),
            pltpu.VMEM((T, D), BF16),
            pltpu.VMEM((T, D), BF16),
            pltpu.VMEM((16, 2, T), I32),
            pltpu.VMEM((D, 3 * D), BF16),
            pltpu.VMEM((D, D), BF16),
            pltpu.VMEM((D, 2048), BF16),
            pltpu.VMEM((2048, D), BF16),
            pltpu.VMEM((T, T), BF16),
            pltpu.VMEM((768, 640), BF16),
            pltpu.VMEM((3, 384, 128), F32),
            pltpu.VMEM((4, 144, T), F32),
            pltpu.VMEM((16, 256, T), BF16),
            pltpu.VMEM((T, D), BF16),
            pltpu.VMEM((4, D, 144), BF16),
            pltpu.VMEM((T, 2 * D), BF16),
            pltpu.VMEM((4, 2 * D, 144), BF16),
            pltpu.VMEM((4, D, 144), BF16),
            pltpu.VMEM((16, 16, T), I32),
            pltpu.VMEM((T, D), BF16),
            pltpu.VMEM((16, SLOT, D), BF16),
            pltpu.VMEM((16, SLOT, D), BF16),
            pltpu.VMEM((16, SLOT, D), BF16),
            pltpu.VMEM((16, SLOT, D), BF16),
            dma((5,)), dma((2,)), dma((2,)), dma((15,)), dma((15,)), dma((15,)), dma((15,)), dma((15,)), dma((15,)),
        ],
        compiler_params=pltpu.CompilerParams(
            vmem_limit_bytes=60 * 1024 * 1024, collective_id=0, has_side_effects=True),
    )(frames, tokens.reshape(T, D), ids, pri, g1, b1, wqkv, qkvb, rel_bias.T, wp, bp, g2, b2, router.T, f1[0], f1b, f2[0], f2b)
    return out.reshape(tokens.shape)


def solution(mesh):
    both = ("grp", "exp")
    one = P(both)
    rep = P()
    in_specs = (P(both, None, None), P("grp", None), one, one) + (rep,) * 10 + (
        P(both, None, None), P(both, None), P(both, None, None), P(both, None))
    return jax.shard_map(shards, mesh=mesh, in_specs=in_specs, out_specs=P(both, None, None), check_vma=False)
```

```python
import math
import jax
import jax.numpy as jnp
from jax import lax
from jax.experimental import pallas as pl
from jax.experimental.pallas import tpu as pltpu
from jax.sharding import PartitionSpec as P

D = 512
HEADS = 16
WIN = 12
STRIPS = 4
T = 576
SLOT = 72
CAP = 720
NEG = -1e30
ROOT = math.sqrt(32.0)
EXPC = math.log2(math.e) / ROOT
F32, BF16, I32 = jnp.float32, jnp.bfloat16, jnp.int32


def iota(shape, dim):
    return lax.broadcasted_iota(I32, shape, dim)


def dot(a, b, dims=((1,), (0,))):
    return lax.dot_general(a, b, (dims, ((), ())), preferred_element_type=F32)


def norm(x, gain, bias):
    mean = jnp.mean(x, axis=-1, keepdims=True)
    c = x - mean
    var = jnp.mean(c * c, axis=-1, keepdims=True)
    return (c * lax.rsqrt(var + 1e-5) * gain + bias).astype(BF16)


def column(row):
    n = row.shape[1]
    if n % 128:
        row = jnp.concatenate([row, jnp.zeros((1, -n % 128), row.dtype)], axis=1)
    return jnp.transpose(jnp.broadcast_to(row, (128, row.shape[1])))[:n, :1]


def build_perm(perm, sr, sc):
    p = iota((T, 1), 0)
    j = p // 144
    w = p - j * 144
    rt = w // 12
    ct = w - rt * 12
    m = rt + sr
    m = jnp.where(m >= 12, m - 12, m)
    c = 12 * j + ct + sc
    c = jnp.where(c >= 48, c - 48, c)
    t = m * 48 + c
    perm[...] = jnp.where(iota((T, T), 1) == t, 1.0, 0.0).astype(BF16)


def build_bias(rel, shifted, spread, table):
    r16 = jnp.concatenate([rel[...] * ROOT, jnp.zeros((16, 640 - 529), F32)], axis=1)
    for r in range(24):
        half, cu = divmod(r, 12)
        s = (-(11 - cu - 23 * half)) % 640
        x = pltpu.roll(r16, s, 1) if s else r16
        hi = x.astype(BF16)
        lo = (x - hi.astype(F32)).astype(BF16)
        shifted[16 * r : 16 * r + 16, :] = hi
        shifted[384 + 16 * r : 384 + 16 * r + 16, :] = lo
    lane = iota((1, 384), 1)
    dr = lane // 12
    want = jnp.where(lane < 276, dr * 23 + lane - dr * 12, -1)
    sel = jnp.where(iota((640, 384), 0) == want, 1.0, 0.0).astype(BF16)
    full = dot(shifted[...], sel)
    full = full[:384] + full[384:]
    for i in range(3):
        spread[i] = full[:, 128 * i : 128 * i + 128]
    for h in range(HEADS):
        g, hh = divmod(h, 4)
        rows = jnp.concatenate([spread[i, pl.ds(h, 24, stride=16), :] for i in range(3)], axis=1)
        for i in range(6):
            start = (11 - 2 * i) * 12
            table[g, 24 * i : 24 * i + 24, 128 * hh : 128 * hh + 128] = rows[:, start : start + 128]
            table[g, 24 * i : 24 * i + 24, 512 + 16 * hh : 528 + 16 * hh] = rows[:, start + 128 : start + 144]


def project_own(xop, wqkv, qkvb, sr, qbd, ko, vo):
    k = dot(xop, wqkv[:, D : 2 * D]) + qkvb[:, D : 2 * D]
    ko[...] = k.astype(BF16)
    bq = column(qkvb[:, :D])
    bv = column(qkvb[:, 2 * D :])
    lane_rt = iota((1, 144), 1) // 12
    in_a = lane_rt >= 12 - sr
    qbd[...] = jnp.zeros_like(qbd)
    for j in range(4):
        xj = xop[144 * j : 144 * j + 144, :]
        qt = dot(wqkv[:, :D], xj, ((0,), (1,))) + bq
        qa = jnp.where(in_a, qt, 0.0).astype(BF16)
        qb = jnp.where(in_a, 0.0, qt).astype(BF16)
        for h in range(HEADS):
            g, hh = divmod(h, 4)
            f = slice(32 * h, 32 * h + 32)
            for off, q in ((0, qa), (128, qb)):
                r = slice(off + 32 * hh, off + 32 * hh + 32)
                qbd[4 * j + g, r, 128 * hh : 128 * hh + 128] = q[f, :128]
                qbd[4 * j + g, r, 512 + 16 * hh : 528 + 16 * hh] = q[f, 128:]
        vo[j] = (dot(wqkv[:, 2 * D :], xj, ((0,), (1,))) + bv).astype(BF16)


def project_halo(first, last, xhp, wqkv, qkvb, sr, ko, vo, kab, vab):
    n = 144 * (last - first)
    rows = slice(144 * first, 144 * last)
    bv = column(qkvb[:, 2 * D :])
    p = iota((n, 1), 0)
    w = p - (p // 144) * 144
    row_a = w // 12 >= 12 - sr
    kh = (dot(xhp, wqkv[:, D : 2 * D]) + qkvb[:, D : 2 * D]).astype(BF16).astype(F32)
    kof = ko[rows, :].astype(F32)
    ka = jnp.where(row_a, kof, kh).astype(BF16)
    kb = jnp.where(row_a, kh, kof).astype(BF16)
    for g in range(4):
        kab[rows, 256 * g : 256 * g + 128] = ka[:, 128 * g : 128 * g + 128]
        kab[rows, 256 * g + 128 : 256 * g + 256] = kb[:, 128 * g : 128 * g + 128]
    in_a = iota((1, 144), 1) // 12 >= 12 - sr
    for j in range(first, last):
        xj = xhp[144 * (j - first) : 144 * (j - first) + 144, :]
        vh = (dot(wqkv[:, 2 * D :], xj, ((0,), (1,))) + bv).astype(BF16).astype(F32)
        vof = vo[j].astype(F32)
        va = jnp.where(in_a, vof, vh).astype(BF16)
        vb = jnp.where(in_a, vh, vof).astype(BF16)
        for h in range(HEADS):
            vab[j, 64 * h : 64 * h + 32, :] = va[32 * h : 32 * h + 32, :]
            vab[j, 64 * h + 32 : 64 * h + 64, :] = vb[32 * h : 32 * h + 32, :]


def attend(j, strip, sr, sc, rows_in, cols_in, qbd, kab, vab, table, att):
    base = strip * 12 + sr

    def cols_of(w):
        ct = w - (w // 12) * 12
        c = 12 * j + ct + sc
        wrapped = c >= 48
        return jnp.where(wrapped, c - 48, c), wrapped

    kpos = iota((144, 1), 0)
    kr = kpos // 12
    kc, kwrap = cols_of(kpos)

    def gid(row, col, wrap):
        region = jnp.where(row < rows_in, jnp.where(col < cols_in, 1, 0), 0)
        return region + jnp.where(wrap, 2, 0)

    row_ka = base - 12 + kr
    row_kb = base + kr
    gid_ka = jnp.where(row_ka < 0, -1, gid(row_ka, kc, kwrap))
    gid_kb = jnp.where(row_kb >= 48, -1, gid(row_kb, kc, kwrap))

    def masks(qpos):
        qr = qpos // 12
        qa = qr >= 12 - sr
        qc, qwrap = cols_of(qpos)
        row_q = jnp.where(qa, base - 12 + qr, base + qr)
        gq = gid(row_q, qc, qwrap)
        want = jnp.where(qa, gid_ka, gid_kb)
        return qa, jnp.where(want == gq, 0.0, NEG)

    lane = iota((1, 128), 1)
    qa_main, m_main = masks(lane)
    lane64 = iota((1, 64), 1)
    qa_rem, m_rem = masks(128 + lane64 - (lane64 // 16) * 16)

    def softmax(s):
        e = jnp.exp2((s - jnp.max(s, axis=0, keepdims=True)) * EXPC)
        return e.astype(BF16), 1.0 / jnp.sum(e, axis=0, keepdims=True)

    for g in range(4):
        s = dot(kab[pl.ds(144 * j, 144), 256 * g : 256 * g + 256], qbd[4 * j + g])
        for pair in range(2):
            h = 4 * g + 2 * pair
            sl = slice(256 * pair, 256 * pair + 256)
            e, inv = softmax(s[:, sl] + table[g, :, sl] + jnp.concatenate([m_main, m_main], axis=1))
            o = dot(vab[j, 64 * h : 64 * h + 128, :], e)
            for i in range(2):
                part = o[64 * i : 64 * i + 64, 128 * i : 128 * i + 128]
                part = jnp.where(qa_main, part[:32], part[32:]) * inv[:, 128 * i : 128 * i + 128]
                att[j, 32 * (h + i) : 32 * (h + i) + 32, :128] = part.astype(BF16)
        e, inv = softmax(s[:, 512:576] + table[g, :, 512:576] + m_rem)
        o = dot(vab[j, 256 * g : 256 * g + 256, :], e)
        for hh in range(4):
            h = 4 * g + hh
            part = jnp.where(qa_rem, o[64 * hh : 64 * hh + 32], o[64 * hh + 32 : 64 * hh + 64]) * inv
            att[j, 32 * h : 32 * h + 32, 128:144] = part[:, 16 * hh : 16 * hh + 16].astype(BF16)


def after_attention(j, att, placed, wp, bp, g2, b2, residual, norm2):
    rows = pl.ds(144 * j, 144)
    projected = dot(att[j], wp[...], ((0,), (0,))) + bp
    res = (placed[rows, :].astype(F32) + projected).astype(BF16)
    residual[rows, :] = res
    norm2[rows, :] = norm(res.astype(F32), g2, b2)


def slot_row(ids_row):
    hits = jnp.where(ids_row == iota((16, T), 0), 1.0, 0.0)
    upper = jnp.where(iota((T, T), 0) < iota((T, T), 1), 1.0, 0.0).astype(BF16)
    before = dot(hits.astype(BF16), upper)
    slot = jnp.sum(before * hits, axis=0, keepdims=True)
    return ids_row * SLOT + slot.astype(I32)


def thresholds(gathered, masked):
    for s in range(16):
        masked[s] = jnp.where(gathered[s, 0:1, :] == iota((16, T), 0), gathered[s, 1:2, :], 1 << 20)

    def step(i, x):
        size = lax.shift_left(jnp.int32(1), 12 - 2 * i)
        cands = [x + size, x + 2 * size, x + 3 * size]
        counts = [jnp.zeros((16, T), I32) for _ in cands]
        for s in range(16):
            m = masked[s]
            counts = [n + jnp.where(m < c, 1, 0) for n, c in zip(counts, cands)]
        for n, c in zip(counts, cands):
            total = jnp.sum(n.astype(F32), axis=1, keepdims=True)
            x = jnp.where(total <= CAP - 1.0, c, x)
        return x

    return lax.fori_loop(0, 7, step, jnp.zeros((16, 1), I32))


def weight_row(norm2, router, ids_row, pri_row, limit):
    hits = ids_row == iota((16, T), 0)
    logits = dot(router, norm2, ((1,), (1,)))
    logit = jnp.sum(jnp.where(hits, logits, 0.0), axis=0, keepdims=True)
    kept = jnp.sum(jnp.where(hits & (pri_row <= limit), 1.0, 0.0), axis=0, keepdims=True)
    return jnp.where(kept > 0.0, 1.0 / (1.0 + jnp.exp(-logit)), 0.0)


def gelu(x):
    z = jnp.abs(x)
    t = 1.0 / (1.0 + (0.3275911 / math.sqrt(2.0)) * z)
    poly = 0.5 * 1.061405429
    for a in (-1.453152027, 1.421413741, -0.284496736, 0.254829592):
        poly = poly * t + 0.5 * a
    tail = poly * t * jnp.exp2((-0.5 * math.log2(math.e)) * (x * x))
    return jnp.maximum(x, 0.0) - z * tail


def mlp(x, w1, b1, w2, b2, step=512):
    acc = None
    for c in range(0, 2048, step):
        h = gelu(dot(x, w1[:, c : c + step]) + b1[:, c : c + step]).astype(BF16)
        y = dot(h, w2[c : c + step, :])
        acc = y if acc is None else acc + y
    return acc + b2


CHUNKS = ((0, 5, 10, 15), (1, 6, 11, 2), (7, 12, 3, 8), (13, 4), (9, 14))


def pack(block, rows, tail):
    for q in range(4):
        block[:, 512 * q : 512 * q + 512] = rows[16 * q : 16 * q + 16].astype(BF16)
    block[:, 2048:] = jnp.concatenate([tail[:, :256], tail[:, 256:]], axis=0).astype(BF16)


def unpack(blocks):
    rows = [b[:, 512 * q : 512 * q + 512] for b in blocks for q in range(4)]
    tails = []
    for b in blocks:
        t = b[:, 2048:].astype(F32)
        tails.append(jnp.concatenate([t[:8], t[8:]], axis=1))
    return jnp.concatenate(rows + [jnp.concatenate(tails, axis=0).astype(BF16)], axis=0)


def pack_all(blocks, rows):
    n = len(blocks)
    for i, block in enumerate(blocks):
        pack(block, rows[64 * i : 64 * i + 64], rows[64 * n + 8 * i : 64 * n + 8 * i + 8])


def pick_rows(peers, dest):
    pieces = [iota((64, T), 0) + SLOT * d for d in peers] + [iota((8, T), 0) + (SLOT * d + 64) for d in peers]
    return jnp.concatenate([jnp.where(p == dest, 1.0, 0.0) for p in pieces], axis=0).astype(BF16)


def pick_columns(peers, dest):
    n = len(peers)
    lane = iota((1, SLOT * n), 1)
    target = jnp.zeros((1, SLOT * n), I32)
    for i, d in enumerate(peers):
        first, second = lane - 64 * i, lane - 64 * n - 8 * i
        target = jnp.where((first >= 0) & (first < 64), first + SLOT * d, target)
        target = jnp.where((second >= 0) & (second < 8), second + (SLOT * d + 64), target)
    return jnp.where(target == dest, 1.0, 0.0).astype(BF16)


def remote(src, dst, send, recv, target):
    return pltpu.make_async_remote_copy(
        src_ref=src, dst_ref=dst, send_sem=send, recv_sem=recv,
        device_id={"exp": target}, device_id_type=pl.DeviceIdType.MESH)


def block_kernel(
    frames, tokens_any, ids1, pri1, g1, b1, wqkv_any, qkvb, rel, wp_any, bp, g2, b2, router, f1_any, f1b, f2_any, f2b,
    out,
    tokens, prev, following, gathered, wqkv, wp, w1, w2,
    perm, shifted, spread, table, qbd, ko, vo, kab, vab, att, masked, residual, outgoing, incoming, served, returned, base, weight_ref, dest_ref, placed, halo, norm2,
    local, halo_send, halo_recv, ids_send, ids_recv, go_send, go_recv, back_send, back_recv,
):
    me = lax.axis_index("exp")
    strip_all = lax.rem(me + 2, 16)
    image = strip_all // STRIPS
    strip = lax.rem(strip_all, STRIPS)
    right, left = lax.rem(me + 1, 16), lax.rem(me + 15, 16)
    barrier = pltpu.get_barrier_semaphore()
    for d in range(1, 16):
        pl.semaphore_signal(barrier, inc=1, device_id={"exp": lax.rem(me + d, 16)}, device_id_type=pl.DeviceIdType.MESH)
    loads = [
        pltpu.make_async_copy(src, dst, local.at[i])
        for i, (src, dst) in enumerate(((tokens_any, tokens), (wqkv_any, wqkv), (wp_any, wp), (f1_any, w1), (f2_any, w2)))
    ]
    for load in loads:
        load.start()
    row = lambda ref: ref[...].reshape(1, ref.shape[0])
    ids_row, pri_row = row(ids1), row(pri1)
    gathered[0, 0:1, :] = ids_row
    gathered[0, 1:2, :] = pri_row
    pl.semaphore_wait(barrier, 15)

    to_left, to_right = [], []
    for i, cols in enumerate((pl.ds(0, 32), pl.ds(32, 16))):
        block = pl.ds(0, 11), cols
        to_left.append(remote(tokens_any.at[block], following.at[block], halo_send.at[i], halo_recv.at[i], left))
        block = pl.ds(1, 11), cols
        to_right.append(remote(tokens_any.at[block], prev.at[block], halo_send.at[2 + i], halo_recv.at[2 + i], right))
    for i in range(2):
        pl.when(strip > 0)(to_left[i].start)
        pl.when(strip < 3)(to_right[i].start)

    ids_copies = [
        remote(gathered.at[0], gathered.at[d], ids_send.at[d - 1], ids_recv.at[d - 1], lax.rem(me + d, 16))
        for d in range(1, 16)
    ]
    for copy in ids_copies:
        copy.start()

    sr, sc, rows_in, cols_in = (frames[image, i] for i in range(4))
    gain1, bias1 = row(g1), row(b1)
    qkv_row = row(qkvb)
    build_perm(perm, sr, sc)
    loads[0].wait()
    flat = tokens[...].reshape(T, D)
    own = norm(flat.astype(F32), gain1, bias1)
    xop = dot(perm[...], own).astype(BF16)
    placed[...] = dot(perm[...], flat).astype(BF16)
    loads[1].wait()
    project_own(xop, wqkv, qkv_row, sr, qbd, ko, vo)
    build_bias(rel, shifted, spread, table)

    halo[:, 32:, :] = jnp.zeros((12, 16, D), BF16)
    bp_row, gain2, bias2 = row(bp), row(g2), row(b2)

    def arrive(i, cols, width):
        pl.when(strip < 3)(to_left[i].wait_recv)
        pl.when(strip > 0)(to_right[i].wait_recv)
        low = iota((12, width, 1), 0) < sr
        have = jnp.where(low, jnp.where(strip < 3, 1, 0), jnp.where(strip > 0, 1, 0)) > 0
        x = jnp.where(low, following[:, cols, :].astype(F32), prev[:, cols, :].astype(F32))
        x = jnp.where(have, x, 0.0).reshape(12 * width, D)
        halo[:, cols, :] = norm(x, gain1, bias1).reshape(12, width, D)

    def window(j, carry):
        attend(j, strip, sr, sc, rows_in, cols_in, qbd, kab, vab, table, att)
        after_attention(j, att, placed, wp, bp_row, gain2, bias2, residual, norm2)
        return carry

    arrive(0, slice(0, 32), 32)
    xhp = dot(perm[0:144, :], halo[...].reshape(T, D)).astype(BF16)
    project_halo(0, 1, xhp, wqkv, qkv_row, sr, ko, vo, kab, vab)
    loads[2].wait()
    window(0, 0)
    arrive(1, slice(32, 48), 16)
    xhp = dot(perm[144:, :], halo[...].reshape(T, D)).astype(BF16)
    project_halo(1, 4, xhp, wqkv, qkv_row, sr, ko, vo, kab, vab)
    lax.fori_loop(1, 4, window, 0)

    relative = lax.rem(ids_row - me + 16, 16)
    dest = slot_row(relative)
    parts = jnp.concatenate([dest // 64, dest - (dest // 64) * 64], axis=0).astype(F32).astype(BF16)
    parts = dot(parts, perm[...], ((1,), (1,)))
    dest_pos = parts[0:1].astype(I32) * 64 + parts[1:2].astype(I32)
    go = [None] + [
        remote(outgoing.at[d], incoming.at[d], go_send.at[d - 1], go_recv.at[d - 1], lax.rem(me + d, 16))
        for d in range(1, 16)
    ]
    back = [None] + [
        remote(served.at[d], returned.at[d], back_send.at[d - 1], back_recv.at[d - 1], lax.rem(me - d + 16, 16))
        for d in range(1, 16)
    ]
    for peers in CHUNKS:
        pack_all([outgoing.at[d] for d in peers], dot(pick_rows(peers, dest_pos), norm2[...]))
        for d in peers:
            if d:
                go[d].start()
    dest_ref[...] = column(dest.astype(F32)).astype(I32)
    norm2_tok = dot(perm[...], norm2[...], ((0,), (0,))).astype(BF16)
    for copy in ids_copies:
        copy.wait_recv()
    limit = thresholds(gathered, masked)
    weight_ref[...] = column(weight_row(norm2_tok, router[...], ids_row, pri_row, limit))
    base[...] = dot(perm[...], residual[...], ((0,), (0,)))
    loads[3].wait()
    loads[4].wait()
    for peers in CHUNKS:
        for d in peers:
            if d:
                go[d].wait_recv()
        x = unpack([incoming.at[d] if d else outgoing.at[0] for d in peers])
        y = mlp(x, w1, f1b, w2, f2b[...])
        pack_all([served.at[d] if d else returned.at[0] for d in peers], y)
        for d in peers:
            if d:
                back[d].start()

    def collect(peers):
        pick = pick_columns(peers, dest_ref[...])
        for d in peers:
            if d:
                back[d].wait_recv()
        return dot(pick, unpack([returned.at[d] for d in peers]))

    early, late = sum(CHUNKS[:3], ()), CHUNKS[4]
    base[...] += weight_ref[...] * collect(early)
    base[...] += weight_ref[...] * collect(CHUNKS[3])
    out[...] = (base[...] + weight_ref[...] * collect(late)).astype(BF16).reshape(12, 48, D)

    for i in range(2):
        pl.when(strip > 0)(to_left[i].wait_send)
        pl.when(strip < 3)(to_right[i].wait_send)
    for copy in ids_copies + go[1:] + back[1:]:
        copy.wait_send()


def shards(tokens, frames, ids, pri, g1, b1, wqkv, qkvb, rel_bias, wp, bp, g2, b2, router, f1, f1b, f2, f2b):
    vm = pl.BlockSpec(memory_space=pltpu.VMEM)
    hbm = pl.BlockSpec(memory_space=pl.ANY)
    specs = [pl.BlockSpec(memory_space=pltpu.SMEM), hbm, vm, vm, vm, vm, hbm, vm, vm, hbm, vm, vm, vm, vm, hbm, vm, hbm, vm]
    dma = pltpu.SemaphoreType.DMA
    out = pl.pallas_call(
        block_kernel,
        out_shape=jax.ShapeDtypeStruct(tokens.shape, BF16),
        in_specs=specs,
        out_specs=vm,
        scratch_shapes=[
            pltpu.VMEM((12, 48, D), BF16),
            pltpu.VMEM((12, 48, D), BF16),
            pltpu.VMEM((12, 48, D), BF16),
            pltpu.VMEM((16, 2, T), I32),
            pltpu.VMEM((D, 3 * D), BF16),
            pltpu.VMEM((D, D), BF16),
            pltpu.VMEM((D, 2048), BF16),
            pltpu.VMEM((2048, D), BF16),
            pltpu.VMEM((T, T), BF16),
            pltpu.VMEM((768, 640), BF16),
            pltpu.VMEM((3, 384, 128), F32),
            pltpu.VMEM((4, 144, T), F32),
            pltpu.VMEM((16, 256, T), BF16),
            pltpu.VMEM((T, D), BF16),
            pltpu.VMEM((4, D, 144), BF16),
            pltpu.VMEM((T, 2 * D), BF16),
            pltpu.VMEM((4, 2 * D, 144), BF16),
            pltpu.VMEM((4, D, 144), BF16),
            pltpu.VMEM((16, 16, T), I32),
            pltpu.VMEM((T, D), BF16),
            pltpu.VMEM((16, 16, 2304), BF16),
            pltpu.VMEM((16, 16, 2304), BF16),
            pltpu.VMEM((16, 16, 2304), BF16),
            pltpu.VMEM((16, 16, 2304), BF16),
            pltpu.VMEM((T, D), F32),
            pltpu.VMEM((T, 1), F32),
            pltpu.VMEM((T, 1), I32),
            pltpu.VMEM((T, D), BF16),
            pltpu.VMEM((12, 48, D), BF16),
            pltpu.VMEM((T, D), BF16),
            dma((5,)), dma((4,)), dma((4,)), dma((15,)), dma((15,)), dma((15,)), dma((15,)), dma((15,)), dma((15,)),
        ],
        compiler_params=pltpu.CompilerParams(
            vmem_limit_bytes=60 * 1024 * 1024, collective_id=0, has_side_effects=True),
    )(frames, tokens, ids, pri, g1, b1, wqkv, qkvb, rel_bias.T, wp, bp, g2, b2, router.T, f1[0], f1b, f2[0], f2b)
    return out


def solution(mesh):
    both = ("grp", "exp")
    one = P(both)
    rep = P()
    in_specs = (P(both, None, None), P("grp", None), one, one) + (rep,) * 10 + (
        P(both, None, None), P(both, None), P(both, None, None), P(both, None))
    return jax.shard_map(shards, mesh=mesh, in_specs=in_specs, out_specs=P(both, None, None), check_vma=False)
```

```python
import math
import jax
import jax.numpy as jnp
from jax import lax
from jax.experimental import pallas as pl
from jax.experimental.pallas import tpu as pltpu
from jax.sharding import PartitionSpec as P

D = 512
HEADS = 16
WIN = 12
STRIPS = 4
T = 576
SLOT = 72
CAP = 720
NEG = -1e30
ROOT = math.sqrt(32.0)
EXPC = math.log2(math.e) / ROOT
F32, BF16, I32 = jnp.float32, jnp.bfloat16, jnp.int32


def iota(shape, dim):
    return lax.broadcasted_iota(I32, shape, dim)


def dot(a, b, dims=((1,), (0,))):
    return lax.dot_general(a, b, (dims, ((), ())), preferred_element_type=F32)


def norm(x, gain, bias):
    mean = jnp.mean(x, axis=-1, keepdims=True)
    c = x - mean
    var = jnp.mean(c * c, axis=-1, keepdims=True)
    return (c * lax.rsqrt(var + 1e-5) * gain + bias).astype(BF16)


def column(row):
    n = row.shape[1]
    if n % 128:
        row = jnp.concatenate([row, jnp.zeros((1, -n % 128), row.dtype)], axis=1)
    return jnp.transpose(jnp.broadcast_to(row, (128, row.shape[1])))[:n, :1]


def build_perm(perm, sr, sc):
    p = iota((T, 1), 0)
    j = p // 144
    w = p - j * 144
    rt = w // 12
    ct = w - rt * 12
    m = rt + sr
    m = jnp.where(m >= 12, m - 12, m)
    c = 12 * j + ct + sc
    c = jnp.where(c >= 48, c - 48, c)
    t = m * 48 + c
    perm[...] = jnp.where(iota((T, T), 1) == t, 1.0, 0.0).astype(BF16)


def build_bias(rel, shifted, spread, table):
    r16 = jnp.concatenate([rel[...] * ROOT, jnp.zeros((16, 640 - 529), F32)], axis=1)
    for r in range(24):
        half, cu = divmod(r, 12)
        s = (-(11 - cu - 23 * half)) % 640
        x = pltpu.roll(r16, s, 1) if s else r16
        hi = x.astype(BF16)
        lo = (x - hi.astype(F32)).astype(BF16)
        shifted[16 * r : 16 * r + 16, :] = hi
        shifted[384 + 16 * r : 384 + 16 * r + 16, :] = lo
    lane = iota((1, 384), 1)
    dr = lane // 12
    want = jnp.where(lane < 276, dr * 23 + lane - dr * 12, -1)
    sel = jnp.where(iota((640, 384), 0) == want, 1.0, 0.0).astype(BF16)
    full = dot(shifted[...], sel)
    full = full[:384] + full[384:]
    for i in range(3):
        spread[i] = full[:, 128 * i : 128 * i + 128]
    for h in range(HEADS):
        g, hh = divmod(h, 4)
        rows = jnp.concatenate([spread[i, pl.ds(h, 24, stride=16), :] for i in range(3)], axis=1)
        for i in range(6):
            start = (11 - 2 * i) * 12
            table[g, 24 * i : 24 * i + 24, 128 * hh : 128 * hh + 128] = rows[:, start : start + 128]
            table[g, 24 * i : 24 * i + 24, 512 + 16 * hh : 528 + 16 * hh] = rows[:, start + 128 : start + 144]


def project_own(xop, wqkv, wvt, bv_ref, qkvb, sr, qbd, ko, vo):
    k = dot(xop, wqkv[:, D : 2 * D]) + qkvb[:, D : 2 * D]
    ko[...] = k.astype(BF16)
    bq = column(qkvb[:, :D])
    bv = column(qkvb[:, 2 * D :])
    bv_ref[...] = bv
    wvt[...] = jnp.transpose(wqkv[:, 2 * D :])
    wqt = jnp.transpose(wqkv[:, :D])
    lane_rt = iota((1, 144), 1) // 12
    in_a = lane_rt >= 12 - sr
    qbd[...] = jnp.zeros_like(qbd)
    for j in range(4):
        xj = xop[144 * j : 144 * j + 144, :]
        qt = dot(wqt, xj, ((1,), (1,))) + bq
        qa = jnp.where(in_a, qt, 0.0).astype(BF16)
        qb = jnp.where(in_a, 0.0, qt).astype(BF16)
        for h in range(HEADS):
            g, hh = divmod(h, 4)
            f = slice(32 * h, 32 * h + 32)
            for off, q in ((0, qa), (128, qb)):
                r = slice(off + 32 * hh, off + 32 * hh + 32)
                qbd[4 * j + g, r, 128 * hh : 128 * hh + 128] = q[f, :128]
                qbd[4 * j + g, r, 512 + 16 * hh : 528 + 16 * hh] = q[f, 128:]
        vo[j] = (dot(wvt[...], xj, ((1,), (1,))) + bv).astype(BF16)


def project_halo(first, last, xhp, wqkv, wvt, bv_ref, qkvb, sr, ko, vo, kab, vab):
    n = 144 * (last - first)
    rows = slice(144 * first, 144 * last)
    bv = bv_ref[...]
    p = iota((n, 1), 0)
    w = p - (p // 144) * 144
    row_a = w // 12 >= 12 - sr
    kh = (dot(xhp, wqkv[:, D : 2 * D]) + qkvb[:, D : 2 * D]).astype(BF16).astype(F32)
    kof = ko[rows, :].astype(F32)
    ka = jnp.where(row_a, kof, kh).astype(BF16)
    kb = jnp.where(row_a, kh, kof).astype(BF16)
    for g in range(4):
        kab[rows, 256 * g : 256 * g + 128] = ka[:, 128 * g : 128 * g + 128]
        kab[rows, 256 * g + 128 : 256 * g + 256] = kb[:, 128 * g : 128 * g + 128]
    in_a = iota((1, 144), 1) // 12 >= 12 - sr
    for j in range(first, last):
        xj = xhp[144 * (j - first) : 144 * (j - first) + 144, :]
        vh = (dot(wvt[...], xj, ((1,), (1,))) + bv).astype(BF16).astype(F32)
        vof = vo[j].astype(F32)
        va = jnp.where(in_a, vof, vh).astype(BF16)
        vb = jnp.where(in_a, vh, vof).astype(BF16)
        for h in range(HEADS):
            vab[j, 64 * h : 64 * h + 32, :] = va[32 * h : 32 * h + 32, :]
            vab[j, 64 * h + 32 : 64 * h + 64, :] = vb[32 * h : 32 * h + 32, :]


def attend(j, strip, sr, sc, rows_in, cols_in, qbd, kab, vab, table, att):
    base = strip * 12 + sr

    def cols_of(w):
        ct = w - (w // 12) * 12
        c = 12 * j + ct + sc
        wrapped = c >= 48
        return jnp.where(wrapped, c - 48, c), wrapped

    kpos = iota((144, 1), 0)
    kr = kpos // 12
    kc, kwrap = cols_of(kpos)

    def gid(row, col, wrap):
        region = jnp.where(row < rows_in, jnp.where(col < cols_in, 1, 0), 0)
        return region + jnp.where(wrap, 2, 0)

    row_ka = base - 12 + kr
    row_kb = base + kr
    gid_ka = jnp.where(row_ka < 0, -1, gid(row_ka, kc, kwrap))
    gid_kb = jnp.where(row_kb >= 48, -1, gid(row_kb, kc, kwrap))

    def masks(qpos):
        qr = qpos // 12
        qa = qr >= 12 - sr
        qc, qwrap = cols_of(qpos)
        row_q = jnp.where(qa, base - 12 + qr, base + qr)
        gq = gid(row_q, qc, qwrap)
        want = jnp.where(qa, gid_ka, gid_kb)
        return qa, jnp.where(want == gq, 0.0, NEG)

    lane = iota((1, 128), 1)
    qa_main, m_main = masks(lane)
    lane64 = iota((1, 64), 1)
    qa_rem, m_rem = masks(128 + lane64 - (lane64 // 16) * 16)

    def softmax(s):
        e = jnp.exp2((s - jnp.max(s, axis=0, keepdims=True)) * EXPC)
        return e.astype(BF16), 1.0 / jnp.sum(e, axis=0, keepdims=True)

    scores = [dot(kab[pl.ds(144 * j, 144), 256 * g : 256 * g + 256], qbd[4 * j + g]) for g in range(4)]
    for g in range(4):
        s = scores[g]
        for pair in range(2):
            h = 4 * g + 2 * pair
            sl = slice(256 * pair, 256 * pair + 256)
            e, inv = softmax(s[:, sl] + table[g, :, sl] + jnp.concatenate([m_main, m_main], axis=1))
            o = dot(vab[j, 64 * h : 64 * h + 128, :], e)
            for i in range(2):
                part = o[64 * i : 64 * i + 64, 128 * i : 128 * i + 128]
                part = jnp.where(qa_main, part[:32], part[32:]) * inv[:, 128 * i : 128 * i + 128]
                att[j, 32 * (h + i) : 32 * (h + i) + 32, :128] = part.astype(BF16)
        e, inv = softmax(s[:, 512:576] + table[g, :, 512:576] + m_rem)
        o = dot(vab[j, 256 * g : 256 * g + 256, :], e)
        for hh in range(4):
            h = 4 * g + hh
            part = jnp.where(qa_rem, o[64 * hh : 64 * hh + 32], o[64 * hh + 32 : 64 * hh + 64]) * inv
            att[j, 32 * h : 32 * h + 32, 128:144] = part[:, 16 * hh : 16 * hh + 16].astype(BF16)


def after_attention(j, att, placed, wp, bp, g2, b2, residual, norm2):
    rows = pl.ds(144 * j, 144)
    projected = dot(att[j], wp[...], ((0,), (0,))) + bp
    res = (placed[rows, :].astype(F32) + projected).astype(BF16)
    residual[rows, :] = res
    norm2[rows, :] = norm(res.astype(F32), g2, b2)


def slot_row(ids_row):
    hits = jnp.where(ids_row == iota((16, T), 0), 1.0, 0.0)
    upper = jnp.where(iota((T, T), 0) < iota((T, T), 1), 1.0, 0.0).astype(BF16)
    before = dot(hits.astype(BF16), upper)
    slot = jnp.sum(before * hits, axis=0, keepdims=True)
    return ids_row * SLOT + slot.astype(I32)


def thresholds(gathered, masked):
    for s in range(16):
        masked[s] = jnp.where(gathered[s, 0:1, :] == iota((16, T), 0), gathered[s, 1:2, :], 1 << 20)

    def step(i, x):
        size = lax.shift_left(jnp.int32(1), 12 - 2 * i)
        cands = [x + size, x + 2 * size, x + 3 * size]
        counts = [jnp.zeros((16, T), I32) for _ in cands]
        for s in range(16):
            m = masked[s]
            counts = [n + jnp.where(m < c, 1, 0) for n, c in zip(counts, cands)]
        for n, c in zip(counts, cands):
            total = jnp.sum(n.astype(F32), axis=1, keepdims=True)
            x = jnp.where(total <= CAP - 1.0, c, x)
        return x

    return lax.fori_loop(0, 7, step, jnp.zeros((16, 1), I32))


def weight_row(norm2, router, ids_row, pri_row, limit):
    hits = ids_row == iota((16, T), 0)
    logits = dot(router, norm2, ((1,), (1,)))
    logit = jnp.sum(jnp.where(hits, logits, 0.0), axis=0, keepdims=True)
    kept = jnp.sum(jnp.where(hits & (pri_row <= limit), 1.0, 0.0), axis=0, keepdims=True)
    return jnp.where(kept > 0.0, 1.0 / (1.0 + jnp.exp(-logit)), 0.0)


def gelu(x):
    z = jnp.abs(x)
    t = 1.0 / (1.0 + (0.3275911 / math.sqrt(2.0)) * z)
    poly = 0.5 * 1.061405429
    for a in (-1.453152027, 1.421413741, -0.284496736, 0.254829592):
        poly = poly * t + 0.5 * a
    tail = poly * t * jnp.exp2((-0.5 * math.log2(math.e)) * (x * x))
    return jnp.maximum(x, 0.0) - z * tail


def mlp(x, w1, b1, w2, b2, step=512):
    acc = None
    for c in range(0, 2048, step):
        h = gelu(dot(x, w1[:, c : c + step]) + b1[:, c : c + step]).astype(BF16)
        y = dot(h, w2[c : c + step, :])
        acc = y if acc is None else acc + y
    return acc + b2


CHUNKS = ((0, 5), (10, 15, 1, 6), (11, 2, 7, 12), (3, 8, 13, 4), (9, 14))
PLACES = (0, 144, 432, 720, 1008)


def pack(block, rows, tail):
    for q in range(4):
        block[:, 512 * q : 512 * q + 512] = rows[16 * q : 16 * q + 16].astype(BF16)
    block[:, 2048:] = jnp.concatenate([tail[:, :256], tail[:, 256:]], axis=0).astype(BF16)


def unpack(blocks):
    rows = [b[:, 512 * q : 512 * q + 512] for b in blocks for q in range(4)]
    tails = []
    for b in blocks:
        t = b[:, 2048:].astype(F32)
        tails.append(jnp.concatenate([t[:8], t[8:]], axis=1))
    return jnp.concatenate(rows + [jnp.concatenate(tails, axis=0).astype(BF16)], axis=0)


def pack_all(blocks, rows):
    n = len(blocks)
    for i, block in enumerate(blocks):
        pack(block, rows[64 * i : 64 * i + 64], rows[64 * n + 8 * i : 64 * n + 8 * i + 8])


def pick_rows(peers, dest):
    pieces = [iota((64, T), 0) + SLOT * d for d in peers] + [iota((8, T), 0) + (SLOT * d + 64) for d in peers]
    return jnp.concatenate([jnp.where(p == dest, 1.0, 0.0) for p in pieces], axis=0).astype(BF16)


def pick_columns(peers, dest):
    n = len(peers)
    lane = iota((1, SLOT * n), 1)
    target = jnp.zeros((1, SLOT * n), I32)
    for i, d in enumerate(peers):
        first, second = lane - 64 * i, lane - 64 * n - 8 * i
        target = jnp.where((first >= 0) & (first < 64), first + SLOT * d, target)
        target = jnp.where((second >= 0) & (second < 8), second + (SLOT * d + 64), target)
    return jnp.where(target == dest, 1.0, 0.0).astype(BF16)


def remote(src, dst, send, recv, target):
    return pltpu.make_async_remote_copy(
        src_ref=src, dst_ref=dst, send_sem=send, recv_sem=recv,
        device_id={"exp": target}, device_id_type=pl.DeviceIdType.MESH)


def block_kernel(
    frames, tokens_any, ids1, pri1, g1, b1, wqkv_any, qkvb, rel, wp_any, bp, g2, b2, router, f1_any, f1b, f2_any, f2b,
    out,
    tokens, prev, following, gathered, wqkv, wp, w1, w2,
    perm, shifted, spread, table, qbd, ko, vo, kab, vab, att, masked, residual, outgoing, incoming, served, returned, base, weight_ref, dest_ref, placed, halo, norm2, wvt, bv_ref, picks,
    local, halo_send, halo_recv, ids_send, ids_recv, go_send, go_recv, back_send, back_recv,
):
    me = lax.axis_index("exp")
    strip_all = lax.rem(me + 2, 16)
    image = strip_all // STRIPS
    strip = lax.rem(strip_all, STRIPS)
    right, left = lax.rem(me + 1, 16), lax.rem(me + 15, 16)
    barrier = pltpu.get_barrier_semaphore()
    for d in range(1, 16):
        pl.semaphore_signal(barrier, inc=1, device_id={"exp": lax.rem(me + d, 16)}, device_id_type=pl.DeviceIdType.MESH)
    loads = [
        pltpu.make_async_copy(src, dst, local.at[i])
        for i, (src, dst) in enumerate(((tokens_any, tokens), (wqkv_any, wqkv), (wp_any, wp), (f1_any, w1), (f2_any, w2)))
    ]
    for load in loads:
        load.start()
    row = lambda ref: ref[...].reshape(1, ref.shape[0])
    ids_row, pri_row = row(ids1), row(pri1)
    gathered[0, 0:1, :] = ids_row
    gathered[0, 1:2, :] = pri_row
    pl.semaphore_wait(barrier, 15)

    to_left, to_right = [], []
    for i, cols in enumerate((pl.ds(0, 32), pl.ds(32, 16))):
        block = pl.ds(0, 11), cols
        to_left.append(remote(tokens_any.at[block], following.at[block], halo_send.at[i], halo_recv.at[i], left))
        block = pl.ds(1, 11), cols
        to_right.append(remote(tokens_any.at[block], prev.at[block], halo_send.at[2 + i], halo_recv.at[2 + i], right))
    for i in range(2):
        pl.when(strip > 0)(to_left[i].start)
        pl.when(strip < 3)(to_right[i].start)

    ids_copies = [
        remote(gathered.at[0], gathered.at[d], ids_send.at[d - 1], ids_recv.at[d - 1], lax.rem(me + d, 16))
        for d in range(1, 16)
    ]
    for copy in ids_copies:
        copy.start()

    sr, sc, rows_in, cols_in = (frames[image, i] for i in range(4))
    gain1, bias1 = row(g1), row(b1)
    qkv_row = row(qkvb)
    build_perm(perm, sr, sc)
    loads[0].wait()
    flat = tokens[...].reshape(T, D)
    own = norm(flat.astype(F32), gain1, bias1)
    xop = dot(perm[...], own).astype(BF16)
    placed[...] = dot(perm[...], flat).astype(BF16)
    loads[1].wait()
    project_own(xop, wqkv, wvt, bv_ref, qkv_row, sr, qbd, ko, vo)
    build_bias(rel, shifted, spread, table)

    relative = lax.rem(ids_row - me + 16, 16)
    dest = slot_row(relative)
    parts = jnp.concatenate([dest // 64, dest - (dest // 64) * 64], axis=0).astype(F32).astype(BF16)
    parts = dot(parts, perm[...], ((1,), (1,)))
    dest_pos = parts[0:1].astype(I32) * 64 + parts[1:2].astype(I32)
    for i, peers in enumerate(CHUNKS):
        picks[PLACES[i] : PLACES[i] + SLOT * len(peers), :] = pick_rows(peers, dest_pos)
    halo[:, 32:, :] = jnp.zeros((12, 16, D), BF16)
    bp_row, gain2, bias2 = row(bp), row(g2), row(b2)

    def arrive(i, cols, width):
        pl.when(strip < 3)(to_left[i].wait_recv)
        pl.when(strip > 0)(to_right[i].wait_recv)
        low = iota((12, width, 1), 0) < sr
        have = jnp.where(low, jnp.where(strip < 3, 1, 0), jnp.where(strip > 0, 1, 0)) > 0
        x = jnp.where(low, following[:, cols, :].astype(F32), prev[:, cols, :].astype(F32))
        x = jnp.where(have, x, 0.0).reshape(12 * width, D)
        halo[:, cols, :] = norm(x, gain1, bias1).reshape(12, width, D)

    def window(j):
        attend(j, strip, sr, sc, rows_in, cols_in, qbd, kab, vab, table, att)
        after_attention(j, att, placed, wp, bp_row, gain2, bias2, residual, norm2)

    arrive(0, slice(0, 32), 32)
    xhp = dot(perm[0:144, :], halo[...].reshape(T, D)).astype(BF16)
    project_halo(0, 1, xhp, wqkv, wvt, bv_ref, qkv_row, sr, ko, vo, kab, vab)
    loads[2].wait()
    window(0)
    arrive(1, slice(32, 48), 16)
    xhp = dot(perm[144:, :], halo[...].reshape(T, D)).astype(BF16)
    project_halo(1, 4, xhp, wqkv, wvt, bv_ref, qkv_row, sr, ko, vo, kab, vab)
    for j in range(1, 4):
        window(j)

    go = [None] + [
        remote(outgoing.at[d], incoming.at[d], go_send.at[d - 1], go_recv.at[d - 1], lax.rem(me + d, 16))
        for d in range(1, 16)
    ]
    back = [None] + [
        remote(served.at[d], returned.at[d], back_send.at[d - 1], back_recv.at[d - 1], lax.rem(me - d + 16, 16))
        for d in range(1, 16)
    ]
    for i, peers in enumerate(CHUNKS):
        pick = picks[PLACES[i] : PLACES[i] + SLOT * len(peers), :]
        pack_all([outgoing.at[d] for d in peers], dot(pick, norm2[...]))
        for d in peers:
            if d:
                go[d].start()
    dest_ref[...] = column(dest.astype(F32)).astype(I32)
    norm2_tok = dot(perm[...], norm2[...], ((0,), (0,))).astype(BF16)
    for copy in ids_copies:
        copy.wait_recv()
    limit = thresholds(gathered, masked)
    weight_ref[...] = column(weight_row(norm2_tok, router[...], ids_row, pri_row, limit))
    base[...] = dot(perm[...], residual[...], ((0,), (0,)))
    loads[3].wait()
    loads[4].wait()
    for peers in CHUNKS:
        for d in peers:
            if d:
                go[d].wait_recv()
        x = unpack([incoming.at[d] if d else outgoing.at[0] for d in peers])
        y = mlp(x, w1, f1b, w2, f2b[...])
        pack_all([served.at[d] if d else returned.at[0] for d in peers], y)
        for d in peers:
            if d:
                back[d].start()

    def collect(peers):
        pick = pick_columns(peers, dest_ref[...])
        for d in peers:
            if d:
                back[d].wait_recv()
        return dot(pick, unpack([returned.at[d] for d in peers]))

    early, late = sum(CHUNKS[:3], ()), CHUNKS[4]
    base[...] += weight_ref[...] * collect(early)
    base[...] += weight_ref[...] * collect(CHUNKS[3])
    out[...] = (base[...] + weight_ref[...] * collect(late)).astype(BF16).reshape(12, 48, D)

    for i in range(2):
        pl.when(strip > 0)(to_left[i].wait_send)
        pl.when(strip < 3)(to_right[i].wait_send)
    for copy in ids_copies + go[1:] + back[1:]:
        copy.wait_send()


def shards(tokens, frames, ids, pri, g1, b1, wqkv, qkvb, rel_bias, wp, bp, g2, b2, router, f1, f1b, f2, f2b):
    vm = pl.BlockSpec(memory_space=pltpu.VMEM)
    hbm = pl.BlockSpec(memory_space=pl.ANY)
    specs = [pl.BlockSpec(memory_space=pltpu.SMEM), hbm, vm, vm, vm, vm, hbm, vm, vm, hbm, vm, vm, vm, vm, hbm, vm, hbm, vm]
    dma = pltpu.SemaphoreType.DMA
    out = pl.pallas_call(
        block_kernel,
        out_shape=jax.ShapeDtypeStruct(tokens.shape, BF16),
        in_specs=specs,
        out_specs=vm,
        scratch_shapes=[
            pltpu.VMEM((12, 48, D), BF16),
            pltpu.VMEM((12, 48, D), BF16),
            pltpu.VMEM((12, 48, D), BF16),
            pltpu.VMEM((16, 2, T), I32),
            pltpu.VMEM((D, 3 * D), BF16),
            pltpu.VMEM((D, D), BF16),
            pltpu.VMEM((D, 2048), BF16),
            pltpu.VMEM((2048, D), BF16),
            pltpu.VMEM((T, T), BF16),
            pltpu.VMEM((768, 640), BF16),
            pltpu.VMEM((3, 384, 128), F32),
            pltpu.VMEM((4, 144, T), F32),
            pltpu.VMEM((16, 256, T), BF16),
            pltpu.VMEM((T, D), BF16),
            pltpu.VMEM((4, D, 144), BF16),
            pltpu.VMEM((T, 2 * D), BF16),
            pltpu.VMEM((4, 2 * D, 144), BF16),
            pltpu.VMEM((4, D, 144), BF16),
            pltpu.VMEM((16, 16, T), I32),
            pltpu.VMEM((T, D), BF16),
            pltpu.VMEM((16, 16, 2304), BF16),
            pltpu.VMEM((16, 16, 2304), BF16),
            pltpu.VMEM((16, 16, 2304), BF16),
            pltpu.VMEM((16, 16, 2304), BF16),
            pltpu.VMEM((T, D), F32),
            pltpu.VMEM((T, 1), F32),
            pltpu.VMEM((T, 1), I32),
            pltpu.VMEM((T, D), BF16),
            pltpu.VMEM((12, 48, D), BF16),
            pltpu.VMEM((T, D), BF16),
            pltpu.VMEM((D, D), BF16),
            pltpu.VMEM((D, 1), F32),
            pltpu.VMEM((16 * SLOT, T), BF16),
            dma((5,)), dma((4,)), dma((4,)), dma((15,)), dma((15,)), dma((15,)), dma((15,)), dma((15,)), dma((15,)),
        ],
        compiler_params=pltpu.CompilerParams(
            vmem_limit_bytes=60 * 1024 * 1024, collective_id=0, has_side_effects=True),
    )(frames, tokens, ids, pri, g1, b1, wqkv, qkvb, rel_bias.T, wp, bp, g2, b2, router.T, f1[0], f1b, f2[0], f2b)
    return out


def solution(mesh):
    both = ("grp", "exp")
    one = P(both)
    rep = P()
    in_specs = (P(both, None, None), P("grp", None), one, one) + (rep,) * 10 + (
        P(both, None, None), P(both, None), P(both, None, None), P(both, None))
    return jax.shard_map(shards, mesh=mesh, in_specs=in_specs, out_specs=P(both, None, None), check_vma=False)
```

```python
import math
import jax
import jax.numpy as jnp
from jax import lax
from jax.experimental import pallas as pl
from jax.experimental.pallas import tpu as pltpu
from jax.sharding import PartitionSpec as P

D = 512
HEADS = 16
WIN = 12
STRIPS = 4
T = 576
SLOT = 72
CAP = 720
NEG = -1e30
ROOT = math.sqrt(32.0)
EXPC = math.log2(math.e) / ROOT
F32, BF16, I32 = jnp.float32, jnp.bfloat16, jnp.int32


def iota(shape, dim):
    return lax.broadcasted_iota(I32, shape, dim)


def dot(a, b, dims=((1,), (0,))):
    return lax.dot_general(a, b, (dims, ((), ())), preferred_element_type=F32)


def norm(x, gain, bias):
    mean = jnp.mean(x, axis=-1, keepdims=True)
    c = x - mean
    var = jnp.mean(c * c, axis=-1, keepdims=True)
    return (c * lax.rsqrt(var + 1e-5) * gain + bias).astype(BF16)


def column(row):
    n = row.shape[1]
    if n % 128:
        row = jnp.concatenate([row, jnp.zeros((1, -n % 128), row.dtype)], axis=1)
    return jnp.transpose(jnp.broadcast_to(row, (128, row.shape[1])))[:n, :1]


def build_perm(perm, sr, sc):
    p = iota((T, 1), 0)
    j = p // 144
    w = p - j * 144
    rt = w // 12
    ct = w - rt * 12
    m = rt + sr
    m = jnp.where(m >= 12, m - 12, m)
    c = 12 * j + ct + sc
    c = jnp.where(c >= 48, c - 48, c)
    t = m * 48 + c
    perm[...] = jnp.where(iota((T, T), 1) == t, 1.0, 0.0).astype(BF16)


def build_bias(rel, shifted, spread, table):
    r16 = jnp.concatenate([rel[...] * ROOT, jnp.zeros((16, 640 - 529), F32)], axis=1)
    for r in range(24):
        half, cu = divmod(r, 12)
        s = (-(11 - cu - 23 * half)) % 640
        x = pltpu.roll(r16, s, 1) if s else r16
        hi = x.astype(BF16)
        lo = (x - hi.astype(F32)).astype(BF16)
        shifted[16 * r : 16 * r + 16, :] = hi
        shifted[384 + 16 * r : 384 + 16 * r + 16, :] = lo
    lane = iota((1, 384), 1)
    dr = lane // 12
    want = jnp.where(lane < 276, dr * 23 + lane - dr * 12, -1)
    sel = jnp.where(iota((640, 384), 0) == want, 1.0, 0.0).astype(BF16)
    full = dot(shifted[...], sel)
    full = full[:384] + full[384:]
    for i in range(3):
        spread[i] = full[:, 128 * i : 128 * i + 128]
    for h in range(HEADS):
        g, hh = divmod(h, 4)
        rows = jnp.concatenate([spread[i, pl.ds(h, 24, stride=16), :] for i in range(3)], axis=1)
        for i in range(6):
            start = (11 - 2 * i) * 12
            table[g, 24 * i : 24 * i + 24, 128 * hh : 128 * hh + 128] = rows[:, start : start + 128]
            table[g, 24 * i : 24 * i + 24, 512 + 16 * hh : 528 + 16 * hh] = rows[:, start + 128 : start + 144]


def project_own(xop, wqkv, wvt, bv_ref, qkvb, sr, qbd, ko, vo):
    k = dot(xop, wqkv[:, D : 2 * D]) + qkvb[:, D : 2 * D]
    ko[...] = k.astype(BF16)
    bq = column(qkvb[:, :D])
    bv = column(qkvb[:, 2 * D :])
    bv_ref[...] = bv
    wvt[...] = jnp.transpose(wqkv[:, 2 * D :])
    wqt = jnp.transpose(wqkv[:, :D])
    lane_rt = iota((1, 144), 1) // 12
    in_a = lane_rt >= 12 - sr
    qbd[...] = jnp.zeros_like(qbd)
    for j in range(4):
        xj = xop[144 * j : 144 * j + 144, :]
        qt = dot(wqt, xj, ((1,), (1,))) + bq
        qa = jnp.where(in_a, qt, 0.0).astype(BF16)
        qb = jnp.where(in_a, 0.0, qt).astype(BF16)
        for h in range(HEADS):
            g, hh = divmod(h, 4)
            f = slice(32 * h, 32 * h + 32)
            for off, q in ((0, qa), (128, qb)):
                r = slice(off + 32 * hh, off + 32 * hh + 32)
                qbd[4 * j + g, r, 128 * hh : 128 * hh + 128] = q[f, :128]
                qbd[4 * j + g, r, 512 + 16 * hh : 528 + 16 * hh] = q[f, 128:]
        vo[j] = (dot(wvt[...], xj, ((1,), (1,))) + bv).astype(BF16)


def project_halo(first, last, xhp, wqkv, wvt, bv_ref, qkvb, sr, ko, vo, kab, vab):
    n = 144 * (last - first)
    rows = slice(144 * first, 144 * last)
    bv = bv_ref[...]
    p = iota((n, 1), 0)
    w = p - (p // 144) * 144
    row_a = w // 12 >= 12 - sr
    kh = (dot(xhp, wqkv[:, D : 2 * D]) + qkvb[:, D : 2 * D]).astype(BF16).astype(F32)
    kof = ko[rows, :].astype(F32)
    ka = jnp.where(row_a, kof, kh).astype(BF16)
    kb = jnp.where(row_a, kh, kof).astype(BF16)
    for g in range(4):
        kab[rows, 256 * g : 256 * g + 128] = ka[:, 128 * g : 128 * g + 128]
        kab[rows, 256 * g + 128 : 256 * g + 256] = kb[:, 128 * g : 128 * g + 128]
    in_a = iota((1, 144), 1) // 12 >= 12 - sr
    for j in range(first, last):
        xj = xhp[144 * (j - first) : 144 * (j - first) + 144, :]
        vh = (dot(wvt[...], xj, ((1,), (1,))) + bv).astype(BF16).astype(F32)
        vof = vo[j].astype(F32)
        va = jnp.where(in_a, vof, vh).astype(BF16)
        vb = jnp.where(in_a, vh, vof).astype(BF16)
        for h in range(HEADS):
            vab[j, 64 * h : 64 * h + 32, :] = va[32 * h : 32 * h + 32, :]
            vab[j, 64 * h + 32 : 64 * h + 64, :] = vb[32 * h : 32 * h + 32, :]


def attend(j, strip, sr, sc, rows_in, cols_in, qbd, kab, vab, table, att):
    base = strip * 12 + sr

    def cols_of(w):
        ct = w - (w // 12) * 12
        c = 12 * j + ct + sc
        wrapped = c >= 48
        return jnp.where(wrapped, c - 48, c), wrapped

    kpos = iota((144, 1), 0)
    kr = kpos // 12
    kc, kwrap = cols_of(kpos)

    def gid(row, col, wrap):
        region = jnp.where(row < rows_in, jnp.where(col < cols_in, 1, 0), 0)
        return region + jnp.where(wrap, 2, 0)

    row_ka = base - 12 + kr
    row_kb = base + kr
    gid_ka = jnp.where(row_ka < 0, -1, gid(row_ka, kc, kwrap))
    gid_kb = jnp.where(row_kb >= 48, -1, gid(row_kb, kc, kwrap))

    def masks(qpos):
        qr = qpos // 12
        qa = qr >= 12 - sr
        qc, qwrap = cols_of(qpos)
        row_q = jnp.where(qa, base - 12 + qr, base + qr)
        gq = gid(row_q, qc, qwrap)
        want = jnp.where(qa, gid_ka, gid_kb)
        return qa, jnp.where(want == gq, 0.0, NEG)

    lane = iota((1, 128), 1)
    qa_main, m_main = masks(lane)
    lane64 = iota((1, 64), 1)
    qa_rem, m_rem = masks(128 + lane64 - (lane64 // 16) * 16)

    def softmax(s):
        e = jnp.exp2((s - jnp.max(s, axis=0, keepdims=True)) * EXPC)
        return e.astype(BF16), 1.0 / jnp.sum(e, axis=0, keepdims=True)

    scores = [dot(kab[pl.ds(144 * j, 144), 256 * g : 256 * g + 256], qbd[4 * j + g]) for g in range(4)]
    for g in range(4):
        s = scores[g]
        for pair in range(2):
            h = 4 * g + 2 * pair
            sl = slice(256 * pair, 256 * pair + 256)
            e, inv = softmax(s[:, sl] + table[g, :, sl] + jnp.concatenate([m_main, m_main], axis=1))
            o = dot(vab[j, 64 * h : 64 * h + 128, :], e)
            for i in range(2):
                part = o[64 * i : 64 * i + 64, 128 * i : 128 * i + 128]
                part = jnp.where(qa_main, part[:32], part[32:]) * inv[:, 128 * i : 128 * i + 128]
                att[j, 32 * (h + i) : 32 * (h + i) + 32, :128] = part.astype(BF16)
        e, inv = softmax(s[:, 512:576] + table[g, :, 512:576] + m_rem)
        o = dot(vab[j, 256 * g : 256 * g + 256, :], e)
        for hh in range(4):
            h = 4 * g + hh
            part = jnp.where(qa_rem, o[64 * hh : 64 * hh + 32], o[64 * hh + 32 : 64 * hh + 64]) * inv
            att[j, 32 * h : 32 * h + 32, 128:144] = part[:, 16 * hh : 16 * hh + 16].astype(BF16)


def after_attention(j, att, placed, wp, bp, g2, b2, residual, norm2):
    rows = pl.ds(144 * j, 144)
    projected = dot(att[j], wp[...], ((0,), (0,))) + bp
    res = (placed[rows, :].astype(F32) + projected).astype(BF16)
    residual[rows, :] = res
    norm2[rows, :] = norm(res.astype(F32), g2, b2)


def slot_row(ids_row):
    hits = jnp.where(ids_row == iota((16, T), 0), 1.0, 0.0)
    upper = jnp.where(iota((T, T), 0) < iota((T, T), 1), 1.0, 0.0).astype(BF16)
    before = dot(hits.astype(BF16), upper)
    slot = jnp.sum(before * hits, axis=0, keepdims=True)
    return ids_row * SLOT + slot.astype(I32)


def thresholds(gathered, masked):
    for s in range(16):
        masked[s] = jnp.where(gathered[s, 0:1, :] == iota((16, T), 0), gathered[s, 1:2, :], 1 << 20)

    def step(i, x):
        size = lax.shift_left(jnp.int32(1), 12 - 2 * i)
        cands = [x + size, x + 2 * size, x + 3 * size]
        counts = [jnp.zeros((16, T), I32) for _ in cands]
        for s in range(16):
            m = masked[s]
            counts = [n + jnp.where(m < c, 1, 0) for n, c in zip(counts, cands)]
        for n, c in zip(counts, cands):
            total = jnp.sum(n.astype(F32), axis=1, keepdims=True)
            x = jnp.where(total <= CAP - 1.0, c, x)
        return x

    return lax.fori_loop(0, 7, step, jnp.zeros((16, 1), I32))


def weight_row(norm2, router, ids_row, pri_row, limit):
    hits = ids_row == iota((16, T), 0)
    logits = dot(router, norm2, ((1,), (1,)))
    logit = jnp.sum(jnp.where(hits, logits, 0.0), axis=0, keepdims=True)
    kept = jnp.sum(jnp.where(hits & (pri_row <= limit), 1.0, 0.0), axis=0, keepdims=True)
    return jnp.where(kept > 0.0, 1.0 / (1.0 + jnp.exp(-logit)), 0.0)


def gelu(x):
    z = jnp.abs(x)
    t = 1.0 / (1.0 + (0.3275911 / math.sqrt(2.0)) * z)
    poly = 0.5 * 1.061405429
    for a in (-1.453152027, 1.421413741, -0.284496736, 0.254829592):
        poly = poly * t + 0.5 * a
    tail = poly * t * jnp.exp2((-0.5 * math.log2(math.e)) * (x * x))
    return jnp.maximum(x, 0.0) - z * tail


def mlp(x, w1, b1, w2, b2, step=512):
    acc = None
    for c in range(0, 2048, step):
        h = gelu(dot(x, w1[:, c : c + step]) + b1[:, c : c + step]).astype(BF16)
        y = dot(h, w2[c : c + step, :])
        acc = y if acc is None else acc + y
    return acc + b2


CHUNKS = ((0, 5), (10, 15, 1, 6), (11, 2, 7, 12), (3, 8, 13, 4), (9, 14))
PLACES = (0, 144, 432, 720, 1008)


def pack(block, rows, tail):
    for q in range(4):
        block[:, 512 * q : 512 * q + 512] = rows[16 * q : 16 * q + 16].astype(BF16)
    block[:, 2048:] = jnp.concatenate([tail[:, :256], tail[:, 256:]], axis=0).astype(BF16)


def unpack(blocks):
    rows = [b[:, 512 * q : 512 * q + 512] for b in blocks for q in range(4)]
    tails = []
    for b in blocks:
        t = b[:, 2048:].astype(F32)
        tails.append(jnp.concatenate([t[:8], t[8:]], axis=1))
    return jnp.concatenate(rows + [jnp.concatenate(tails, axis=0).astype(BF16)], axis=0)


def pack_all(blocks, rows):
    n = len(blocks)
    for i, block in enumerate(blocks):
        pack(block, rows[64 * i : 64 * i + 64], rows[64 * n + 8 * i : 64 * n + 8 * i + 8])


def pick_rows(peers, dest):
    pieces = [iota((64, T), 0) + SLOT * d for d in peers] + [iota((8, T), 0) + (SLOT * d + 64) for d in peers]
    return jnp.concatenate([jnp.where(p == dest, 1.0, 0.0) for p in pieces], axis=0).astype(BF16)


def pick_columns(peers, dest):
    n = len(peers)
    lane = iota((1, SLOT * n), 1)
    target = jnp.zeros((1, SLOT * n), I32)
    for i, d in enumerate(peers):
        first, second = lane - 64 * i, lane - 64 * n - 8 * i
        target = jnp.where((first >= 0) & (first < 64), first + SLOT * d, target)
        target = jnp.where((second >= 0) & (second < 8), second + (SLOT * d + 64), target)
    return jnp.where(target == dest, 1.0, 0.0).astype(BF16)


def remote(src, dst, send, recv, target):
    return pltpu.make_async_remote_copy(
        src_ref=src, dst_ref=dst, send_sem=send, recv_sem=recv,
        device_id={"exp": target}, device_id_type=pl.DeviceIdType.MESH)


def block_kernel(
    frames, tokens_any, ids1, pri1, g1, b1, wqkv_any, qkvb, rel, wp_any, bp, g2, b2, router, f1_any, f1b, f2_any, f2b,
    out,
    tokens, prev, following, gathered, wqkv, wp, w1, w2,
    perm, shifted, spread, table, qbd, ko, vo, kab, vab, att, masked, residual, outgoing, incoming, served, returned, base, weight_ref, dest_ref, placed, halo, norm2, wvt, bv_ref, picks,
    local, halo_send, halo_recv, ids_send, ids_recv, go_send, go_recv, back_send, back_recv,
):
    me = lax.axis_index("exp")
    strip_all = lax.rem(me + 2, 16)
    image = strip_all // STRIPS
    strip = lax.rem(strip_all, STRIPS)
    right, left = lax.rem(me + 1, 16), lax.rem(me + 15, 16)
    barrier = pltpu.get_barrier_semaphore()
    for d in range(1, 16):
        pl.semaphore_signal(barrier, inc=1, device_id={"exp": lax.rem(me + d, 16)}, device_id_type=pl.DeviceIdType.MESH)
    loads = [
        pltpu.make_async_copy(src, dst, local.at[i])
        for i, (src, dst) in enumerate(((tokens_any, tokens), (wqkv_any, wqkv), (wp_any, wp), (f1_any, w1), (f2_any, w2)))
    ]
    for load in loads:
        load.start()
    row = lambda ref: ref[...].reshape(1, ref.shape[0])
    ids_row, pri_row = row(ids1), row(pri1)
    gathered[0, 0:1, :] = ids_row
    gathered[0, 1:2, :] = pri_row
    pl.semaphore_wait(barrier, 15)

    to_left, to_right = [], []
    for i, cols in enumerate((pl.ds(0, 32), pl.ds(32, 16))):
        block = pl.ds(0, 11), cols
        to_left.append(remote(tokens_any.at[block], following.at[block], halo_send.at[i], halo_recv.at[i], left))
        block = pl.ds(1, 11), cols
        to_right.append(remote(tokens_any.at[block], prev.at[block], halo_send.at[2 + i], halo_recv.at[2 + i], right))
    for i in range(2):
        pl.when(strip > 0)(to_left[i].start)
        pl.when(strip < 3)(to_right[i].start)

    ids_copies = [
        remote(gathered.at[0], gathered.at[d], ids_send.at[d - 1], ids_recv.at[d - 1], lax.rem(me + d, 16))
        for d in range(1, 16)
    ]
    for copy in ids_copies:
        copy.start()

    sr, sc, rows_in, cols_in = (frames[image, i] for i in range(4))
    gain1, bias1 = row(g1), row(b1)
    qkv_row = row(qkvb)
    build_perm(perm, sr, sc)
    loads[0].wait()
    flat = tokens[...].reshape(T, D)
    own = norm(flat.astype(F32), gain1, bias1)
    xop = dot(perm[...], own).astype(BF16)
    placed[...] = dot(perm[...], flat).astype(BF16)
    loads[1].wait()
    project_own(xop, wqkv, wvt, bv_ref, qkv_row, sr, qbd, ko, vo)
    build_bias(rel, shifted, spread, table)

    relative = lax.rem(ids_row - me + 16, 16)
    dest = slot_row(relative)
    parts = jnp.concatenate([dest // 64, dest - (dest // 64) * 64], axis=0).astype(F32).astype(BF16)
    parts = dot(parts, perm[...], ((1,), (1,)))
    dest_pos = parts[0:1].astype(I32) * 64 + parts[1:2].astype(I32)
    for i, peers in enumerate(CHUNKS):
        picks[PLACES[i] : PLACES[i] + SLOT * len(peers), :] = pick_rows(peers, dest_pos)
    halo[:, 32:, :] = jnp.zeros((12, 16, D), BF16)
    bp_row, gain2, bias2 = row(bp), row(g2), row(b2)

    def arrive(i, cols, width):
        pl.when(strip < 3)(to_left[i].wait_recv)
        pl.when(strip > 0)(to_right[i].wait_recv)
        low = iota((12, width, 1), 0) < sr
        have = jnp.where(low, jnp.where(strip < 3, 1, 0), jnp.where(strip > 0, 1, 0)) > 0
        x = jnp.where(low, following[:, cols, :].astype(F32), prev[:, cols, :].astype(F32))
        x = jnp.where(have, x, 0.0).reshape(12 * width, D)
        halo[:, cols, :] = norm(x, gain1, bias1).reshape(12, width, D)

    def window(j):
        attend(j, strip, sr, sc, rows_in, cols_in, qbd, kab, vab, table, att)
        after_attention(j, att, placed, wp, bp_row, gain2, bias2, residual, norm2)

    arrive(0, slice(0, 32), 32)
    xhp = dot(perm[0:144, :], halo[...].reshape(T, D)).astype(BF16)
    project_halo(0, 1, xhp, wqkv, wvt, bv_ref, qkv_row, sr, ko, vo, kab, vab)
    loads[2].wait()
    window(0)
    arrive(1, slice(32, 48), 16)
    xhp = dot(perm[144:, :], halo[...].reshape(T, D)).astype(BF16)
    project_halo(1, 4, xhp, wqkv, wvt, bv_ref, qkv_row, sr, ko, vo, kab, vab)
    for j in range(1, 4):
        attend(j, strip, sr, sc, rows_in, cols_in, qbd, kab, vab, table, att)
    for j in range(1, 4):
        after_attention(j, att, placed, wp, bp_row, gain2, bias2, residual, norm2)

    go = [None] + [
        remote(outgoing.at[d], incoming.at[d], go_send.at[d - 1], go_recv.at[d - 1], lax.rem(me + d, 16))
        for d in range(1, 16)
    ]
    back = [None] + [
        remote(served.at[d], returned.at[d], back_send.at[d - 1], back_recv.at[d - 1], lax.rem(me - d + 16, 16))
        for d in range(1, 16)
    ]
    for i, peers in enumerate(CHUNKS):
        pick = picks[PLACES[i] : PLACES[i] + SLOT * len(peers), :]
        pack_all([outgoing.at[d] for d in peers], dot(pick, norm2[...]))
        for d in peers:
            if d:
                go[d].start()
    dest_ref[...] = column(dest.astype(F32)).astype(I32)
    norm2_tok = dot(perm[...], norm2[...], ((0,), (0,))).astype(BF16)
    for copy in ids_copies:
        copy.wait_recv()
    limit = thresholds(gathered, masked)
    weight_ref[...] = column(weight_row(norm2_tok, router[...], ids_row, pri_row, limit))
    base[...] = dot(perm[...], residual[...], ((0,), (0,)))
    loads[3].wait()
    loads[4].wait()
    for peers in CHUNKS:
        for d in peers:
            if d:
                go[d].wait_recv()
        x = unpack([incoming.at[d] if d else outgoing.at[0] for d in peers])
        y = mlp(x, w1, f1b, w2, f2b[...])
        pack_all([served.at[d] if d else returned.at[0] for d in peers], y)
        for d in peers:
            if d:
                back[d].start()

    def collect(peers):
        pick = pick_columns(peers, dest_ref[...])
        for d in peers:
            if d:
                back[d].wait_recv()
        return dot(pick, unpack([returned.at[d] for d in peers]))

    early, late = sum(CHUNKS[:3], ()), CHUNKS[4]
    base[...] += weight_ref[...] * collect(early)
    base[...] += weight_ref[...] * collect(CHUNKS[3])
    out[...] = (base[...] + weight_ref[...] * collect(late)).astype(BF16).reshape(12, 48, D)

    for i in range(2):
        pl.when(strip > 0)(to_left[i].wait_send)
        pl.when(strip < 3)(to_right[i].wait_send)
    for copy in ids_copies + go[1:] + back[1:]:
        copy.wait_send()


def shards(tokens, frames, ids, pri, g1, b1, wqkv, qkvb, rel_bias, wp, bp, g2, b2, router, f1, f1b, f2, f2b):
    vm = pl.BlockSpec(memory_space=pltpu.VMEM)
    hbm = pl.BlockSpec(memory_space=pl.ANY)
    specs = [pl.BlockSpec(memory_space=pltpu.SMEM), hbm, vm, vm, vm, vm, hbm, vm, vm, hbm, vm, vm, vm, vm, hbm, vm, hbm, vm]
    dma = pltpu.SemaphoreType.DMA
    out = pl.pallas_call(
        block_kernel,
        out_shape=jax.ShapeDtypeStruct(tokens.shape, BF16),
        in_specs=specs,
        out_specs=vm,
        scratch_shapes=[
            pltpu.VMEM((12, 48, D), BF16),
            pltpu.VMEM((12, 48, D), BF16),
            pltpu.VMEM((12, 48, D), BF16),
            pltpu.VMEM((16, 2, T), I32),
            pltpu.VMEM((D, 3 * D), BF16),
            pltpu.VMEM((D, D), BF16),
            pltpu.VMEM((D, 2048), BF16),
            pltpu.VMEM((2048, D), BF16),
            pltpu.VMEM((T, T), BF16),
            pltpu.VMEM((768, 640), BF16),
            pltpu.VMEM((3, 384, 128), F32),
            pltpu.VMEM((4, 144, T), F32),
            pltpu.VMEM((16, 256, T), BF16),
            pltpu.VMEM((T, D), BF16),
            pltpu.VMEM((4, D, 144), BF16),
            pltpu.VMEM((T, 2 * D), BF16),
            pltpu.VMEM((4, 2 * D, 144), BF16),
            pltpu.VMEM((4, D, 144), BF16),
            pltpu.VMEM((16, 16, T), I32),
            pltpu.VMEM((T, D), BF16),
            pltpu.VMEM((16, 16, 2304), BF16),
            pltpu.VMEM((16, 16, 2304), BF16),
            pltpu.VMEM((16, 16, 2304), BF16),
            pltpu.VMEM((16, 16, 2304), BF16),
            pltpu.VMEM((T, D), F32),
            pltpu.VMEM((T, 1), F32),
            pltpu.VMEM((T, 1), I32),
            pltpu.VMEM((T, D), BF16),
            pltpu.VMEM((12, 48, D), BF16),
            pltpu.VMEM((T, D), BF16),
            pltpu.VMEM((D, D), BF16),
            pltpu.VMEM((D, 1), F32),
            pltpu.VMEM((16 * SLOT, T), BF16),
            dma((5,)), dma((4,)), dma((4,)), dma((15,)), dma((15,)), dma((15,)), dma((15,)), dma((15,)), dma((15,)),
        ],
        compiler_params=pltpu.CompilerParams(
            vmem_limit_bytes=60 * 1024 * 1024, collective_id=0, has_side_effects=True),
    )(frames, tokens, ids, pri, g1, b1, wqkv, qkvb, rel_bias.T, wp, bp, g2, b2, router.T, f1[0], f1b, f2[0], f2b)
    return out


def solution(mesh):
    both = ("grp", "exp")
    one = P(both)
    rep = P()
    in_specs = (P(both, None, None), P("grp", None), one, one) + (rep,) * 10 + (
        P(both, None, None), P(both, None), P(both, None, None), P(both, None))
    return jax.shard_map(shards, mesh=mesh, in_specs=in_specs, out_specs=P(both, None, None), check_vma=False)
```
